32 devices in a mesh: group: 4 (over y, core), fsdp: 8 (over z, x).
Axes of the slice: x: 2, y: 2, z: 4, core: 2. Of those that a mesh axis runs over, the one named last changes fastest.
Arguments:
- tokens: bfloat16 [4, 3072, 4096], P('group', 'fsdp'), may hold values from -6 to 6
- targets: bfloat16 [4, 3072, 512], P('group', 'fsdp'), may hold values from -6 to 6
- params: float32 [4, 4096, 512], P('group', 'fsdp'), may hold values from -6 to 6
- momentum: float32 [4, 4096, 512], P('group', 'fsdp'), may hold values from -6 to 6
- push_weight: float32 [4], P('group'), may hold values from 0.5 to 2
Outputs:
- new_params: float32 [4, 4096, 512], P('group', 'fsdp')
- new_momentum: float32 [4, 4096, 512], P('group', 'fsdp')
The draws below stay inside these ranges and needn't reach their ends.
All inputs are finite; a program needn't handle non-finite values.
Results may differ from the reference program's by a relative error of at most 0.0031.
Values may be sent and summed in bfloat16 or wider, within the bound.
No kernel may reach another device: no remote copies, remote signals or barrier semaphores. Data moves between devices by JAX's collectives and lax.ppermute only.
A program may use at most 64 MiB of HBM per device.

```python
import math
import jax
import jax.numpy as jnp
from jax import lax

D = 4096
KVW = 512
STEPS = 2
TOKENS = 3072
N_GROUP = 4


def block_levels(key, extent, pieces, least, largest):
    level, own = 1.0, jax.random.fold_in(key, 6)
    for axis_at, blocks in pieces:
        draws = jnp.exp(jax.random.uniform(jax.random.fold_in(own, axis_at), (blocks,), jnp.float32, least / len(pieces), largest / len(pieces)))
        level = level * jnp.repeat(draws, extent[axis_at] // blocks).reshape([-1 if axis == axis_at else 1 for axis in range(len(extent))])
    return level


def noise(stream_key, shape, scale, bound, shards=(), dtype=jnp.bfloat16):
    entries = scale * jax.random.normal(stream_key, shape, jnp.float32)
    if shards:
        entries = entries * block_levels(stream_key, shape, shards, -0.22, 0.18)
    return jnp.clip(entries, -bound, bound).astype(dtype)


def setup_inputs(seed: int = 0) -> dict:
    key_of = jax.random.split(jax.random.key(seed), 6)
    return {
        "tokens": noise(key_of[0], (N_GROUP, TOKENS, D), 1.0, 6.0, ((0, 4), (1, 8))),
        "targets": noise(key_of[1], (N_GROUP, TOKENS, KVW), 1.0, 6.0, ((0, 4), (1, 8))),
        "params": noise(key_of[2], (N_GROUP, D, KVW), 1.0, 6.0, ((0, 4), (1, 8)), jnp.float32),
        "momentum": noise(key_of[3], (N_GROUP, D, KVW), 1.0, 6.0, ((0, 4), (1, 8)), jnp.float32),
        "push_weight": jnp.clip(jnp.exp(math.log(2.0) - 1.3862944 * jax.random.uniform(key_of[4], (N_GROUP,), jnp.float32) ** block_levels(key_of[4], (N_GROUP,), ((0, 4),), -0.2, 0.2)), 0.5, 2.0),
    }


def reference(tokens, targets, params, momentum, push_weight):
    key_scale = D ** -0.5
    state = params
    moment = momentum
    weight = push_weight

    def one_group(operands):
        inputs, target, debiased = operands
        raw_keys = jnp.dot(inputs, debiased, preferred_element_type=jnp.float32)
        residual = key_scale * raw_keys - target.astype(jnp.float32)
        grad_out = (key_scale * residual).astype(jnp.bfloat16)
        return jnp.dot(inputs.T, grad_out, preferred_element_type=jnp.float32)

    for round_index in range(STEPS):
        debiased = (state / weight[:, None, None]).astype(jnp.bfloat16)
        gradient = lax.map(one_group, (tokens, targets, debiased))
        moment = 0.9 * moment + gradient
        state = state - 0.2 * moment
        distance = 2 ** round_index
        state = 0.5 * state + 0.5 * jnp.roll(state, distance, axis=0)
        weight = 0.5 * weight + 0.5 * jnp.roll(weight, distance, axis=0)
    return state / weight[:, None, None], moment
```

```python
import jax
import jax.numpy as jnp
from jax import lax
from jax.sharding import PartitionSpec as P

STEPS = 2
CHUNKS = 2


def from_behind(value, axis, steps):
    count = lax.axis_size(axis)
    pairs = [(source, (source + steps) % count) for source in range(count)]
    return lax.ppermute(value, axis, pairs)


def shards(tokens, targets, params, momentum, push_weight):
    inputs = tokens[0]
    rows, width = inputs.shape
    features = params.shape[2]
    count = lax.axis_size("fsdp")
    lane = lax.rem(lax.axis_index("fsdp"), 2)
    swap = [(i, i ^ 1) for i in range(count)]
    lines = [list(range(0, count, 2)), list(range(1, count, 2))]
    key_scale = width ** (-0.5)
    part = features // CHUNKS

    def chunk(array, c):
        return array[:, c * part : (c + 1) * part]

    weights = [push_weight]
    for step in range(STEPS):
        weights.append(0.5 * weights[-1] + 0.5 * from_behind(weights[-1], "group", 2**step))

    state = [chunk(params[0], c) for c in range(CHUNKS)]
    moment = [chunk(momentum[0], c) for c in range(CHUNKS)]
    target = [chunk(targets[0], c).astype(jnp.float32) for c in range(CHUNKS)]

    columns = inputs.reshape(rows, count // 2, 2, width // count)
    mine = lax.dynamic_index_in_dim(columns, lane, 2, keepdims=False)
    theirs = lax.dynamic_index_in_dim(columns, 1 - lane, 2, keepdims=False)
    mine = mine.reshape(rows, width // 2)
    theirs = lax.ppermute(theirs.reshape(rows, width // 2), "fsdp", swap)

    for step in range(STEPS):
        for c in range(CHUNKS):
            debiased = (state[c] / weights[step][0]).astype(jnp.bfloat16)
            gathered = lax.all_gather(
                debiased, "fsdp", axis=0, tiled=True, axis_index_groups=lines
            )
            before = state[c] - (0.2 * 0.9) * moment[c]
            before = 0.5 * (before + from_behind(before, "group", 2**step))
            own = key_scale * jnp.dot(mine, gathered, preferred_element_type=jnp.float32)
            own = own - target[c]
            other = key_scale * jnp.dot(theirs, gathered, preferred_element_type=jnp.float32)
            sent = jnp.concatenate([other, own]).astype(jnp.bfloat16)
            got = lax.ppermute(sent, "fsdp", swap).astype(jnp.float32)
            own_grad = (key_scale * (own + got[:rows])).astype(jnp.bfloat16)
            other_grad = (key_scale * (other + got[rows:])).astype(jnp.bfloat16)
            contract = (((0,), (0,)), ((), ()))
            partial = lax.dot_general(
                mine, own_grad, contract, preferred_element_type=jnp.float32
            ) + lax.dot_general(theirs, other_grad, contract, preferred_element_type=jnp.float32)
            gradient = lax.psum_scatter(
                partial.astype(jnp.bfloat16),
                "fsdp",
                scatter_dimension=0,
                axis_index_groups=lines,
                tiled=True,
            )
            behind = from_behind(gradient, "group", 2**step).astype(jnp.float32)
            gradient = gradient.astype(jnp.float32)
            moment[c] = 0.9 * moment[c] + gradient
            state[c] = before - 0.1 * (gradient + behind)
    new_params = jnp.concatenate([s / weights[STEPS][0] for s in state], axis=1)
    return new_params[None], jnp.concatenate(moment, axis=1)[None]


def solution(mesh):
    return jax.shard_map(
        shards,
        mesh=mesh,
        in_specs=(
            P("group", "fsdp", None),
            P("group", "fsdp", None),
            P("group", "fsdp", None),
            P("group", "fsdp", None),
            P("group"),
        ),
        out_specs=(P("group", "fsdp", None), P("group", "fsdp", None)),
        check_vma=False,
    )
```

```python
import jax
import jax.numpy as jnp
from jax import lax
from jax.sharding import PartitionSpec as P

STEPS = 2
CHUNKS = 2


def from_behind(value, axis, steps):
    count = lax.axis_size(axis)
    pairs = [(source, (source + steps) % count) for source in range(count)]
    return lax.ppermute(value, axis, pairs)


def shards(tokens, targets, params, momentum, push_weight):
    inputs = tokens[0]
    rows, width = inputs.shape
    features = params.shape[2]
    count = lax.axis_size("fsdp")
    lane = lax.rem(lax.axis_index("fsdp"), 2)
    swap = [(i, i ^ 1) for i in range(count)]
    half = count // 2
    order = list(range(0, half, 2)) + list(range(1, half, 2))
    lines = [[2 * place + side for place in order] for side in range(2)]
    key_scale = width ** (-0.5)
    part = features // CHUNKS

    def chunk(array, c):
        return array[:, c * part : (c + 1) * part]

    weights = [push_weight]
    for step in range(STEPS):
        weights.append(0.5 * weights[-1] + 0.5 * from_behind(weights[-1], "group", 2**step))

    state = [chunk(params[0], c) for c in range(CHUNKS)]
    moment = [chunk(momentum[0], c) for c in range(CHUNKS)]
    target = [chunk(targets[0], c).astype(jnp.float32) for c in range(CHUNKS)]

    block = width // count

    def half_columns(side):
        pieces = [
            lax.dynamic_slice_in_dim(inputs, (2 * place + side) * block, block, 1)
            for place in order
        ]
        return jnp.concatenate(pieces, axis=1)

    theirs = lax.ppermute(half_columns(1 - lane), "fsdp", swap)
    mine = half_columns(lane)

    for step in range(STEPS):
        for c in range(CHUNKS):
            debiased = (state[c] / weights[step][0]).astype(jnp.bfloat16)
            gathered = lax.all_gather(
                debiased, "fsdp", axis=0, tiled=True, axis_index_groups=lines
            )
            before = state[c] - (0.2 * 0.9) * moment[c]
            before = 0.5 * (before + from_behind(before, "group", 2**step))
            own = key_scale * jnp.dot(mine, gathered, preferred_element_type=jnp.float32)
            own = own - target[c]
            other = key_scale * jnp.dot(theirs, gathered, preferred_element_type=jnp.float32)
            sent = jnp.concatenate([other, own]).astype(jnp.bfloat16)
            got = lax.ppermute(sent, "fsdp", swap).astype(jnp.float32)
            own_grad = (key_scale * (own + got[:rows])).astype(jnp.bfloat16)
            other_grad = (key_scale * (other + got[rows:])).astype(jnp.bfloat16)
            contract = (((0,), (0,)), ((), ()))
            partial = lax.dot_general(
                mine, own_grad, contract, preferred_element_type=jnp.float32
            ) + lax.dot_general(theirs, other_grad, contract, preferred_element_type=jnp.float32)
            gradient = lax.psum_scatter(
                partial.astype(jnp.bfloat16),
                "fsdp",
                scatter_dimension=0,
                axis_index_groups=lines,
                tiled=True,
            )
            behind = from_behind(gradient, "group", 2**step).astype(jnp.float32)
            gradient = gradient.astype(jnp.float32)
            moment[c] = 0.9 * moment[c] + gradient
            state[c] = before - 0.1 * (gradient + behind)
            state[c], moment[c] = lax.optimization_barrier((state[c], moment[c]))
    new_params = jnp.concatenate([s / weights[STEPS][0] for s in state], axis=1)
    return new_params[None], jnp.concatenate(moment, axis=1)[None]


def solution(mesh):
    return jax.shard_map(
        shards,
        mesh=mesh,
        in_specs=(
            P("group", "fsdp", None),
            P("group", "fsdp", None),
            P("group", "fsdp", None),
            P("group", "fsdp", None),
            P("group"),
        ),
        out_specs=(P("group", "fsdp", None), P("group", "fsdp", None)),
        check_vma=False,
    )
```

```python
import jax
import jax.numpy as jnp
from jax import lax
from jax.sharding import PartitionSpec as P

STEPS = 2
CHUNKS = 2


def from_behind(value, axis, steps):
    count = lax.axis_size(axis)
    pairs = [(source, (source + steps) % count) for source in range(count)]
    return lax.ppermute(value, axis, pairs)


def shards(tokens, targets, params, momentum, push_weight):
    inputs = tokens[0]
    rows, width = inputs.shape
    features = params.shape[2]
    count = lax.axis_size("fsdp")
    half = count // 2
    block = width // count
    place = lax.div(lax.axis_index("fsdp"), 2)
    lane = lax.rem(lax.axis_index("fsdp"), 2)
    swap = [(i, i ^ 1) for i in range(count)]
    key_scale = width ** (-0.5)
    part = features // CHUNKS
    contract = (((0,), (0,)), ((), ()))

    def chunk(array, c):
        return array[:, c * part : (c + 1) * part]

    def half_columns(side):
        pieces = []
        for back in range(half):
            start = (2 * lax.rem(place - back + half, half) + side) * block
            pieces.append(lax.dynamic_slice_in_dim(inputs, start, block, 1))
        return jnp.concatenate(pieces, axis=1)

    theirs = lax.ppermute(half_columns(1 - lane), "fsdp", swap)
    mine = half_columns(lane)

    weights = [push_weight]
    for step in range(STEPS):
        weights.append(0.5 * weights[-1] + 0.5 * from_behind(weights[-1], "group", 2**step))

    state = [chunk(params[0], c) for c in range(CHUNKS)]
    moment = [chunk(momentum[0], c) for c in range(CHUNKS)]
    target = [chunk(targets[0], c).astype(jnp.float32) for c in range(CHUNKS)]

    for step in range(STEPS):
        before = []
        for c in range(CHUNKS):
            own = state[c] - (0.2 * 0.9) * moment[c]
            before.append(0.5 * (own + from_behind(own, "group", 2**step)))
        for c in range(CHUNKS):
            rows_in = (state[c] / weights[step][0]).astype(jnp.bfloat16)
            own = -target[c]
            other = 0.0
            for back in range(half):
                columns = slice(back * block, (back + 1) * block)
                own = own + key_scale * jnp.dot(
                    mine[:, columns], rows_in, preferred_element_type=jnp.float32
                )
                other = other + key_scale * jnp.dot(
                    theirs[:, columns], rows_in, preferred_element_type=jnp.float32
                )
                if back < half - 1:
                    rows_in = from_behind(rows_in, "fsdp", 2)
            sent = jnp.concatenate([other, own]).astype(jnp.bfloat16)
            got = lax.ppermute(sent, "fsdp", swap).astype(jnp.float32)
            own_grad = (key_scale * (own + got[:rows])).astype(jnp.bfloat16)
            other_grad = (key_scale * (other + got[rows:])).astype(jnp.bfloat16)

            def partial(back):
                columns = slice(back * block, (back + 1) * block)
                return lax.dot_general(
                    mine[:, columns], own_grad, contract, preferred_element_type=jnp.float32
                ) + lax.dot_general(
                    theirs[:, columns], other_grad, contract, preferred_element_type=jnp.float32
                )

            total = partial(1)
            for back in range(2, half + 1):
                total = from_behind(total.astype(jnp.bfloat16), "fsdp", 2)
                total = total.astype(jnp.float32) + partial(back % half)
            behind = from_behind(total.astype(jnp.bfloat16), "group", 2**step)
            moment[c] = 0.9 * moment[c] + total
            state[c] = before[c] - 0.1 * (total + behind.astype(jnp.float32))
            state[c], moment[c] = lax.optimization_barrier((state[c], moment[c]))
    new_params = jnp.concatenate([s / weights[STEPS][0] for s in state], axis=1)
    return new_params[None], jnp.concatenate(moment, axis=1)[None]


def solution(mesh):
    return jax.shard_map(
        shards,
        mesh=mesh,
        in_specs=(
            P("group", "fsdp", None),
            P("group", "fsdp", None),
            P("group", "fsdp", None),
            P("group", "fsdp", None),
            P("group"),
        ),
        out_specs=(P("group", "fsdp", None), P("group", "fsdp", None)),
        check_vma=False,
    )
```

```python
import jax
import jax.numpy as jnp
from jax import lax
from jax.sharding import PartitionSpec as P

STEPS = 2


def from_behind(value, axis, steps):
    count = lax.axis_size(axis)
    pairs = [(source, (source + steps) % count) for source in range(count)]
    return lax.ppermute(value, axis, pairs)


def tie(*values):
    return lax.optimization_barrier(values)


def shards(tokens, targets, params, momentum, push_weight):
    inputs = tokens[0]
    rows, width = inputs.shape
    features = params.shape[2]
    count = lax.axis_size("fsdp")
    half = count // 2
    block = width // count
    place = lax.div(lax.axis_index("fsdp"), 2)
    lane = lax.rem(lax.axis_index("fsdp"), 2)
    swap = [(i, i ^ 1) for i in range(count)]
    key_scale = width ** (-0.5)
    part = features // 2
    contract = (((0,), (0,)), ((), ()))
    wide = jnp.float32
    narrow = jnp.bfloat16

    def chunk(array, c):
        return array[:, c * part : (c + 1) * part]

    def half_columns(side):
        pieces = []
        for back in range(half):
            start = (2 * lax.rem(place - back + half, half) + side) * block
            pieces.append(lax.dynamic_slice_in_dim(inputs, start, block, 1))
        return jnp.concatenate(pieces, axis=1)

    outgoing, params, momentum = tie(half_columns(1 - lane), params, momentum)
    theirs = lax.ppermute(outgoing, "fsdp", swap)
    mine = half_columns(lane)

    def debias(numerators, weight):
        return (numerators / weight[0]).astype(narrow)

    def column_block(array, back):
        return array[:, back * block : (back + 1) * block]

    def gather(rows_in):
        pieces = [rows_in]
        for _ in range(half - 1):
            pieces.append(from_behind(pieces[-1], "fsdp", 2))
        return pieces

    def product(left, pieces, total):
        for back, piece in enumerate(pieces):
            total = total + key_scale * jnp.dot(
                column_block(left, back), piece, preferred_element_type=wide
            )
        return total

    def partial(own_grad, other_grad, back):
        return lax.dot_general(
            column_block(mine, back), own_grad, contract, preferred_element_type=wide
        ) + lax.dot_general(
            column_block(theirs, back), other_grad, contract, preferred_element_type=wide
        )

    weights = [push_weight]
    for step in range(STEPS):
        weights.append(0.5 * weights[-1] + 0.5 * from_behind(weights[-1], "group", 2**step))

    state = [chunk(params[0], c) for c in range(2)]
    moment = [chunk(momentum[0], c) for c in range(2)]
    target = [chunk(targets[0], c).astype(wide) for c in range(2)]

    for step in range(STEPS):
        last = step == STEPS - 1
        if step == 0:
            debiased = [debias(state[c], weights[step]) for c in range(2)]
        pieces = [gather(debiased[c]) for c in range(2)]
        if step == 0:
            whole = params[0] - (0.2 * 0.9) * momentum[0]
            whole, *weights = tie(whole, *weights)
            before = 0.5 * (whole + from_behind(whole, "group", 2**step))
            before = [chunk(before, c) for c in range(2)]
        else:
            before = [state[c] - (0.2 * 0.9) * moment[c] for c in range(2)]
            before = list(tie(*before))
            got = from_behind(before[0], "group", 2**step)
            got, before[1] = tie(got, before[1])
            before[0] = 0.5 * (before[0] + got)
            before[1] = 0.5 * (before[1] + from_behind(before[1], "group", 2**step))

        own = [product(mine, pieces[c], -target[c]) for c in range(2)]
        other = [product(theirs, pieces[c], 0.0) for c in range(2)]
        got = []
        for c in range(2):
            sent = jnp.concatenate([other[c], own[c]]).astype(narrow)
            if c == 0:
                sent, before[0] = tie(sent, before[0])
            got.append(lax.ppermute(sent, "fsdp", swap))

        def gradients(c):
            received = got[c].astype(wide)
            own_grad = (key_scale * (own[c] + received[:rows])).astype(narrow)
            other_grad = (key_scale * (other[c] + received[rows:])).astype(narrow)
            return own_grad, other_grad

        grads = gradients(0)
        first = from_behind(partial(*grads, 1).astype(narrow), "fsdp", 2)
        first, got[1], before[1] = tie(first, got[1], before[1])
        grads = [grads, gradients(1)]
        second = from_behind(partial(*grads[1], 1).astype(narrow), "fsdp", 2)
        arrived = [first, second]
        for back in range(2, half):
            for c in range(2):
                total = arrived[c].astype(wide) + partial(*grads[c], back)
                arrived[c] = from_behind(total.astype(narrow), "fsdp", 2)
        for c in range(2):
            total = arrived[c].astype(wide) + partial(*grads[c], 0)
            behind = from_behind(total.astype(narrow), "group", 2**step)
            if c == 0 and last:
                behind, arrived[1] = tie(behind, arrived[1])
            moment[c] = 0.9 * moment[c] + total
            state[c] = before[c] - 0.1 * (total + behind.astype(wide))
            if not last:
                state[c], moment[c] = tie(state[c], moment[c])
                debiased[c] = debias(state[c], weights[step + 1])
                if c == 0:
                    debiased[c], arrived[1] = tie(debiased[c], arrived[1])
    new_params = jnp.concatenate([s / weights[STEPS][0] for s in state], axis=1)
    return new_params[None], jnp.concatenate(moment, axis=1)[None]


def solution(mesh):
    return jax.shard_map(
        shards,
        mesh=mesh,
        in_specs=(
            P("group", "fsdp", None),
            P("group", "fsdp", None),
            P("group", "fsdp", None),
            P("group", "fsdp", None),
            P("group"),
        ),
        out_specs=(P("group", "fsdp", None), P("group", "fsdp", None)),
        check_vma=False,
    )
```

```python
import jax
import jax.numpy as jnp
from jax import lax
from jax.experimental import pallas as pl
from jax.experimental.pallas import tpu as pltpu
from jax.sharding import PartitionSpec as P

STEPS = 2


def from_behind(value, axis, steps):
    count = lax.axis_size(axis)
    pairs = [(source, (source + steps) % count) for source in range(count)]
    return lax.ppermute(value, axis, pairs)


def tie(*values):
    return lax.optimization_barrier(values)


def select_columns(inputs, starts, block):
    rows = inputs.shape[0]
    count = starts.shape[0]

    def kernel(starts_ref, inputs_ref, out_ref, sems):
        copies = []
        for i in range(count):
            start = pl.multiple_of(starts_ref[i], block)
            copies.append(
                pltpu.make_async_copy(
                    inputs_ref.at[:, pl.ds(start, block)],
                    out_ref.at[:, pl.ds(i * block, block)],
                    sems.at[i],
                )
            )
        for copy in copies:
            copy.start()
        for copy in copies:
            copy.wait()

    size = rows * count * block * inputs.dtype.itemsize
    return pl.pallas_call(
        kernel,
        out_shape=jax.ShapeDtypeStruct((rows, count * block), inputs.dtype),
        in_specs=[
            pl.BlockSpec(memory_space=pltpu.SMEM),
            pl.BlockSpec(memory_space=pl.ANY),
        ],
        out_specs=pl.BlockSpec(memory_space=pl.ANY),
        scratch_shapes=[pltpu.SemaphoreType.DMA((count,))],
        cost_estimate=pl.CostEstimate(flops=0, bytes_accessed=2 * size, transcendentals=0),
    )(starts, inputs)


def shards(tokens, targets, params, momentum, push_weight):
    inputs = tokens[0]
    rows, width = inputs.shape
    features = params.shape[2]
    count = lax.axis_size("fsdp")
    half = count // 2
    block = width // count
    place = lax.div(lax.axis_index("fsdp"), 2)
    lane = lax.rem(lax.axis_index("fsdp"), 2)
    swap = [(i, i ^ 1) for i in range(count)]
    key_scale = width ** (-0.5)
    part = features // 2
    contract = (((0,), (0,)), ((), ()))
    wide = jnp.float32
    narrow = jnp.bfloat16

    def chunk(array, c):
        return array[:, c * part : (c + 1) * part]

    def half_columns(side):
        pieces = []
        for back in range(half):
            start = (2 * lax.rem(place - back + half, half) + side) * block
            pieces.append(lax.dynamic_slice_in_dim(inputs, start, block, 1))
        return jnp.concatenate(pieces, axis=1)

    behind = [lax.rem(place - back + half, half) for back in range(half)]
    starts = jnp.stack([(2 * at + 1 - lane) * block for at in behind])
    outgoing = select_columns(inputs, starts.astype(jnp.int32), block)
    outgoing, params, momentum, push_weight = tie(outgoing, params, momentum, push_weight)
    theirs = lax.ppermute(outgoing, "fsdp", swap)
    mine = half_columns(lane)

    def debias(numerators, weight):
        return (numerators / weight[0]).astype(narrow)

    def column_block(array, back):
        return array[:, back * block : (back + 1) * block]

    def gather(pieces):
        while len(pieces) < half:
            pieces.append(from_behind(pieces[-1], "fsdp", 2))
        return pieces

    def product(left, pieces, total):
        for back, piece in enumerate(pieces):
            total = total + key_scale * jnp.dot(
                column_block(left, back), piece, preferred_element_type=wide
            )
        return total

    def partial(own_grad, other_grad, back):
        return lax.dot_general(
            column_block(mine, back), own_grad, contract, preferred_element_type=wide
        ) + lax.dot_general(
            column_block(theirs, back), other_grad, contract, preferred_element_type=wide
        )

    weights = [push_weight]
    for step in range(STEPS):
        weights.append(0.5 * weights[-1] + 0.5 * from_behind(weights[-1], "group", 2**step))

    state = [chunk(params[0], c) for c in range(2)]
    moment = [chunk(momentum[0], c) for c in range(2)]
    target = [chunk(targets[0], c).astype(wide) for c in range(2)]

    for step in range(STEPS):
        last = step == STEPS - 1
        if step == 0:
            debiased = [[debias(state[c], weights[step])] for c in range(2)]
        pieces = [gather(debiased[c]) for c in range(2)]
        if step == 0:
            whole = params[0] - (0.2 * 0.9) * momentum[0]
            whole, *weights = tie(whole, *weights)
            before = 0.5 * (whole + from_behind(whole, "group", 2**step))
            before = [chunk(before, c) for c in range(2)]
        else:
            before = [state[c] - (0.2 * 0.9) * moment[c] for c in range(2)]
            before = list(tie(*before))
            got = from_behind(before[0].astype(narrow), "group", 2**step)
            got, before[1] = tie(got, before[1])
            before[0] = 0.5 * (before[0] + got.astype(wide))
            got = from_behind(before[1].astype(narrow), "group", 2**step)
            before[1] = 0.5 * (before[1] + got.astype(wide))

        own = [product(mine, pieces[c], -target[c]) for c in range(2)]
        other = [product(theirs, pieces[c], 0.0) for c in range(2)]
        got = []
        for c in range(2):
            sent = jnp.concatenate([other[c], own[c]]).astype(narrow)
            if c == 0:
                sent, before[0] = tie(sent, before[0])
            got.append(lax.ppermute(sent, "fsdp", swap))

        def gradients(c):
            received = got[c].astype(wide)
            own_grad = (key_scale * (own[c] + received[:rows])).astype(narrow)
            other_grad = (key_scale * (other[c] + received[rows:])).astype(narrow)
            return own_grad, other_grad

        grads = gradients(0)
        first = from_behind(partial(*grads, 1).astype(narrow), "fsdp", 2)
        first, got[1], before[1] = tie(first, got[1], before[1])
        grads = [grads, gradients(1)]
        second = from_behind(partial(*grads[1], 1).astype(narrow), "fsdp", 2)
        arrived = [first, second]
        for back in range(2, half):
            for c in range(2):
                total = arrived[c].astype(wide) + partial(*grads[c], back)
                arrived[c] = from_behind(total.astype(narrow), "fsdp", 2)
        for c in range(2):
            total = arrived[c].astype(wide) + partial(*grads[c], 0)
            behind = from_behind(total.astype(narrow), "group", 2**step)
            if c == 0 and last:
                behind, arrived[1] = tie(behind, arrived[1])
            moment[c] = 0.9 * moment[c] + total
            state[c] = before[c] - 0.1 * (total + behind.astype(wide))
            if not last:
                state[c], moment[c] = tie(state[c], moment[c])
                debiased[c] = debias(state[c], weights[step + 1])
                if c == 0:
                    debiased[c] = [debiased[c], from_behind(debiased[c], "fsdp", 2)]
                    debiased[c][1], arrived[1] = tie(debiased[c][1], arrived[1])
                else:
                    debiased[c] = [debiased[c]]
    new_params = jnp.concatenate([s / weights[STEPS][0] for s in state], axis=1)
    return new_params[None], jnp.concatenate(moment, axis=1)[None]


def solution(mesh):
    return jax.shard_map(
        shards,
        mesh=mesh,
        in_specs=(
            P("group", "fsdp", None),
            P("group", "fsdp", None),
            P("group", "fsdp", None),
            P("group", "fsdp", None),
            P("group"),
        ),
        out_specs=(P("group", "fsdp", None), P("group", "fsdp", None)),
        check_vma=False,
    )
```

```python
import jax
import jax.numpy as jnp
from jax import lax
from jax.experimental import pallas as pl
from jax.experimental.pallas import tpu as pltpu
from jax.sharding import PartitionSpec as P

STEPS = 2


def from_behind(value, axis, steps):
    count = lax.axis_size(axis)
    pairs = [(source, (source + steps) % count) for source in range(count)]
    return lax.ppermute(value, axis, pairs)


def after(value, *earlier):
    return lax.optimization_barrier((value, *earlier))[0]


def select_columns(inputs, starts, block):
    rows = inputs.shape[0]
    count = starts.shape[0]

    def kernel(starts_ref, inputs_ref, out_ref):
        out_ref[...] = inputs_ref[...]

    size = rows * count * block * inputs.dtype.itemsize
    return pl.pallas_call(
        kernel,
        out_shape=jax.ShapeDtypeStruct((rows, count * block), inputs.dtype),
        grid_spec=pltpu.PrefetchScalarGridSpec(
            num_scalar_prefetch=1,
            grid=(count,),
            in_specs=[pl.BlockSpec((rows, block), lambda i, starts: (0, starts[i]))],
            out_specs=pl.BlockSpec((rows, block), lambda i, starts: (0, i)),
        ),
        cost_estimate=pl.CostEstimate(flops=0, bytes_accessed=2 * size, transcendentals=0),
    )(starts, inputs)


def shards(tokens, targets, params, momentum, push_weight):
    inputs = tokens[0]
    rows, width = inputs.shape
    features = params.shape[2]
    count = lax.axis_size("fsdp")
    half = count // 2
    block = width // count
    place = lax.div(lax.axis_index("fsdp"), 2)
    lane = lax.rem(lax.axis_index("fsdp"), 2)
    swap = [(i, i ^ 1) for i in range(count)]
    key_scale = width ** (-0.5)
    part = features // 2
    contract = (((0,), (0,)), ((), ()))
    wide = jnp.float32
    narrow = jnp.bfloat16

    def chunk(array, c):
        return array[:, c * part : (c + 1) * part]

    def half_columns(side):
        pieces = []
        for back in range(half):
            start = (2 * lax.rem(place - back + half, half) + side) * block
            pieces.append(lax.dynamic_slice_in_dim(inputs, start, block, 1))
        return jnp.concatenate(pieces, axis=1)

    behind = [lax.rem(place - back + half, half) for back in range(half)]
    starts = jnp.stack([2 * at + 1 - lane for at in behind])
    outgoing = select_columns(inputs, starts.astype(jnp.int32), block)
    params = after(params, outgoing)
    momentum = after(momentum, outgoing)
    theirs = lax.ppermute(outgoing, "fsdp", swap)
    mine = half_columns(lane)

    def debias(numerators, weight):
        return (numerators / weight[0]).astype(narrow)

    def column_block(array, back):
        return array[:, back * block : (back + 1) * block]

    def gather(pieces):
        while len(pieces) < half:
            pieces.append(from_behind(pieces[-1], "fsdp", 2))
        return pieces

    def product(left, pieces, total):
        for back, piece in enumerate(pieces):
            total = total + key_scale * jnp.dot(
                column_block(left, back), piece, preferred_element_type=wide
            )
        return total

    def partial(own_grad, other_grad, back):
        return lax.dot_general(
            column_block(mine, back), own_grad, contract, preferred_element_type=wide
        ) + lax.dot_general(
            column_block(theirs, back), other_grad, contract, preferred_element_type=wide
        )

    state = [chunk(params[0], c) for c in range(2)]
    moment = [chunk(momentum[0], c) for c in range(2)]
    target = [chunk(targets[0], c).astype(wide) for c in range(2)]

    weights = [push_weight]
    debiased = [[debias(state[c], push_weight)] for c in range(2)]

    for step in range(STEPS):
        last = step == STEPS - 1
        pieces = debiased
        for back in range(1, half):
            for c in range(2):
                if len(pieces[c]) == back:
                    pieces[c].append(from_behind(pieces[c][-1], "fsdp", 2))
        if step == 0:
            whole = params[0] - (0.2 * 0.9) * momentum[0]
            got = from_behind(whole, "group", 2**step)
            before = 0.5 * (whole + got)
            before = [chunk(before, c) for c in range(2)]
            ready = [got, got]
        else:
            pieces[0][-1] = after(pieces[0][-1], pieces[1][-3])
            own = [state[c] - (0.2 * 0.9) * moment[c] for c in range(2)]
            late = after(own[0].astype(narrow), own[1])
            before, ready = [], []
            for c in range(2):
                got = from_behind(late, "group", 2**step)
                before.append(0.5 * (own[c] + got.astype(wide)))
                ready.append(got)
                late = after(own[1].astype(narrow), got)

        own = [product(mine, pieces[c], -target[c]) for c in range(2)]
        other = [product(theirs, pieces[c], 0.0) for c in range(2)]
        got = []
        for c in range(2):
            sent = jnp.concatenate([other[c], own[c]]).astype(narrow)
            sent = after(sent, ready[c])
            got.append(lax.ppermute(sent, "fsdp", swap))
            if step == 0 and c == 0:
                weights[0] = after(weights[0], sent)
                for hop in range(STEPS):
                    came = from_behind(weights[-1], "group", 2**hop)
                    weights.append(0.5 * (weights[-1] + came))

        def gradients(c):
            received = got[c].astype(wide)
            own_grad = (key_scale * (own[c] + received[:rows])).astype(narrow)
            other_grad = (key_scale * (other[c] + received[rows:])).astype(narrow)
            return own_grad, other_grad

        grads = gradients(0)
        def pass_on(total):
            total = total.astype(narrow)
            return total, from_behind(total, "fsdp", 2)

        def add(c, back):
            return arrived[c].astype(wide) + partial(*grads[c], back)

        arrived = [pass_on(after(partial(*grads, 1).astype(narrow), sent))[1]]
        grads = [grads]
        gone, arrived[0] = pass_on(add(0, 2))
        got[1] = after(got[1], gone, *weights)
        grads.append(gradients(1))
        arrived.append(pass_on(partial(*grads[1], 1))[1])
        for back in range(3, half + 1):
            if back < half:
                arrived[0] = pass_on(add(0, back))[1]
            arrived[1] = pass_on(add(1, back - 1))[1]
        for c in range(2):
            total = add(c, 0)
            behind = from_behind(total.astype(narrow), "group", 2**step)
            if c == 0 and last:
                arrived[1] = after(arrived[1], behind)
            moment[c] = 0.9 * moment[c] + total
            state[c] = before[c] - 0.1 * (total + behind.astype(wide))
            if not last:
                debiased[c] = [debias(state[c], weights[step + 1])]
                if c == 0:
                    debiased[c].append(from_behind(debiased[c][0], "fsdp", 2))
                    arrived[1] = after(arrived[1], debiased[c][1])
    new_params = jnp.concatenate([s / weights[STEPS][0] for s in state], axis=1)
    return new_params[None], jnp.concatenate(moment, axis=1)[None]


def solution(mesh):
    return jax.shard_map(
        shards,
        mesh=mesh,
        in_specs=(
            P("group", "fsdp", None),
            P("group", "fsdp", None),
            P("group", "fsdp", None),
            P("group", "fsdp", None),
            P("group"),
        ),
        out_specs=(P("group", "fsdp", None), P("group", "fsdp", None)),
        check_vma=False,
    )
```

```python
import jax
import jax.numpy as jnp
from jax import lax
from jax.sharding import PartitionSpec as P

STEPS = 2
CHUNKS = 4
OCCUPANCY = {"line": 2.7, "pair": 4.0, "group": 2.6}
LATENCY = 3.5
SWAP_ENDS = 36.0


def from_behind(value, axis, steps):
    count = lax.axis_size(axis)
    pairs = [(source, (source + steps) % count) for source in range(count)]
    return lax.ppermute(value, axis, pairs)


def after(value, *earlier):
    return lax.optimization_barrier((value, *earlier))[0]


def issue_order(half):
    hops = ["line"] * (half - 1)
    plan = (hops + ["pair"] + hops + ["group"]) * STEPS
    free = {"line": 0.0, "pair": SWAP_ENDS, "group": 0.0}
    ready = [0.01 * c for c in range(CHUNKS)]
    at = [0] * CHUNKS
    order = []
    while len(order) < CHUNKS * len(plan):
        c = min((c for c in range(CHUNKS) if at[c] < len(plan)), key=lambda c: ready[c])
        link = plan[at[c]]
        start = max(ready[c], free[link])
        free[link] = start + OCCUPANCY[link]
        ready[c] = free[link] + LATENCY
        at[c] += 1
        order.append(c)
    return order


def shards(tokens, targets, params, momentum, push_weight):
    inputs = tokens[0]
    rows, width = inputs.shape
    features = params.shape[2]
    count = lax.axis_size("fsdp")
    half = count // 2
    block = width // count
    place = lax.div(lax.axis_index("fsdp"), 2)
    lane = lax.rem(lax.axis_index("fsdp"), 2)
    key_scale = width ** (-0.5)
    part = features // CHUNKS
    contract = (((0,), (0,)), ((), ()))
    wide = jnp.float32
    narrow = jnp.bfloat16
    issued = []

    def send(value, link, steps=1):
        if issued:
            value = after(value, issued[-1])
        issued.append(value)
        if link == "pair":
            return lax.ppermute(value, "fsdp", [(i, i ^ 1) for i in range(count)])
        if link == "line":
            return from_behind(value, "fsdp", 2)
        return from_behind(value, "group", steps)

    def chunk(array, c):
        return array[:, c * part : (c + 1) * part]

    def half_columns(side):
        pieces = []
        for back in range(half):
            start = (2 * lax.rem(place - back + half, half) + side) * block
            pieces.append(lax.dynamic_slice_in_dim(inputs, start, block, 1))
        return jnp.concatenate(pieces, axis=1)

    def column_block(array, back):
        return array[:, back * block : (back + 1) * block]

    def product(left, pieces, total):
        for back, piece in enumerate(pieces):
            total = total + key_scale * jnp.dot(
                column_block(left, back), piece, preferred_element_type=wide
            )
        return total

    outgoing = half_columns(1 - lane)
    theirs = send(outgoing, "pair")
    params = after(params, outgoing)
    momentum = after(momentum, outgoing)
    mine = half_columns(lane)
    weights = [push_weight]
    kept = [[] for _ in range(STEPS)]
    passed = {}
    results = [jnp.zeros_like(params[0]), jnp.zeros_like(momentum[0])]

    def stream(c):
        state = chunk(params[0], c)
        moment = chunk(momentum[0], c)
        target = chunk(targets[0], c).astype(wide)
        for step in range(STEPS):
            kept[step].append(state - (0.2 * 0.9) * moment)
            pieces = [(state / weights[step][0]).astype(narrow)]
            for _ in range(half - 1):
                pieces.append((yield pieces[-1], "line"))
            own = product(mine, pieces, -target)
            other = product(theirs, pieces, 0.0)
            received = yield jnp.concatenate([other, own]).astype(narrow), "pair"
            received = received.astype(wide)
            own_grad = (key_scale * (own + received[:rows])).astype(narrow)
            other_grad = (key_scale * (other + received[rows:])).astype(narrow)

            def partial(back):
                return lax.dot_general(
                    column_block(mine, back), own_grad, contract, preferred_element_type=wide
                ) + lax.dot_general(
                    column_block(theirs, back), other_grad, contract, preferred_element_type=wide
                )

            total = partial(1)
            for back in range(2, half + 1):
                arrived = yield total.astype(narrow), "line"
                total = arrived.astype(wide) + partial(back % half)
            behind = yield total.astype(narrow), "group"
            moment = 0.9 * moment + total
            mixed = 0.5 * (kept[step][c] + chunk(passed[step], c).astype(wide))
            state = mixed - 0.1 * (total + behind.astype(wide))
        fresh = [state / weights[STEPS][0], moment]
        for i in range(2):
            results[i] = lax.dynamic_update_slice(results[i], fresh[i], (0, c * part))
        yield None, None

    streams = [stream(c) for c in range(CHUNKS)]
    waiting = [next(running) for running in streams]
    groups_sent = [0] * CHUNKS
    for c in issue_order(half):
        value, link = waiting[c]
        result = send(value, link, 2 ** groups_sent[c])
        groups_sent[c] += link == "group"
        if link == "pair" and len(weights) == 1:
            for hop in range(STEPS):
                came = send(weights[-1], "group", 2**hop)
                weights.append(0.5 * (weights[-1] + came))
        waiting[c] = (result, link)
        pending = streams[c]
        waiting[c] = pending.send(result)
        for step in range(STEPS):
            if step not in passed and len(kept[step]) == CHUNKS:
                if step == 0:
                    passed[step] = send(jnp.concatenate(kept[0], axis=1), "group", 1)
                else:
                    whole = jnp.concatenate(kept[step], axis=1).astype(narrow)
                    passed[step] = send(whole, "group", 2**step)
    return results[0][None], results[1][None]


def solution(mesh):
    return jax.shard_map(
        shards,
        mesh=mesh,
        in_specs=(
            P("group", "fsdp", None),
            P("group", "fsdp", None),
            P("group", "fsdp", None),
            P("group", "fsdp", None),
            P("group"),
        ),
        out_specs=(P("group", "fsdp", None), P("group", "fsdp", None)),
        check_vma=False,
    )
```

```python
import jax
import jax.numpy as jnp
from jax import lax
from jax.sharding import PartitionSpec as P

STEPS = 2
CHUNKS = 4
OCCUPANCY = {"line": 5.5, "pair": 7.9, "group": 4.0}
LATENCY = 3.2
PREPARE = 0.6
SWAP_ENDS = 36.0


def from_behind(value, axis, steps):
    count = lax.axis_size(axis)
    pairs = [(source, (source + steps) % count) for source in range(count)]
    return lax.ppermute(value, axis, pairs)


def after(value, *earlier):
    return lax.optimization_barrier((value, *earlier))[0]


def issue_order(half):
    hops = ["line"] * (half - 1)
    plan = (hops + ["pair"] + hops + ["group"]) * STEPS
    free = {"line": 0.0, "pair": SWAP_ENDS, "group": 0.0, "core": 0.0}
    ready = [0.01 * c for c in range(CHUNKS)]
    at = [0] * CHUNKS
    order = []
    while len(order) < CHUNKS * len(plan):
        c = min((c for c in range(CHUNKS) if at[c] < len(plan)), key=lambda c: ready[c])
        link = plan[at[c]]
        free["core"] = max(ready[c], free["core"]) + PREPARE
        start = max(free["core"], free[link])
        free[link] = start + OCCUPANCY[link] * 2 / CHUNKS
        ready[c] = free[link] + LATENCY
        at[c] += 1
        order.append(c)
    return order


def shards(tokens, targets, params, momentum, push_weight):
    inputs = tokens[0]
    rows, width = inputs.shape
    features = params.shape[2]
    count = lax.axis_size("fsdp")
    half = count // 2
    block = width // count
    place = lax.div(lax.axis_index("fsdp"), 2)
    lane = lax.rem(lax.axis_index("fsdp"), 2)
    key_scale = width ** (-0.5)
    part = features // CHUNKS
    contract = (((0,), (0,)), ((), ()))
    wide = jnp.float32
    narrow = jnp.bfloat16
    issued = []

    def send(value, link, steps=1):
        if issued:
            value = after(value, issued[-1])
        issued.append(value)
        if link == "pair":
            return lax.ppermute(value, "fsdp", [(i, i ^ 1) for i in range(count)])
        if link == "line":
            return from_behind(value, "fsdp", 2)
        return from_behind(value, "group", steps)

    def chunk(array, c):
        return array[:, c * part : (c + 1) * part]

    def half_columns(side):
        pieces = []
        for back in range(half):
            start = (2 * lax.rem(place - back + half, half) + side) * block
            pieces.append(lax.dynamic_slice_in_dim(inputs, start, block, 1))
        return jnp.concatenate(pieces, axis=1)

    def column_block(back):
        return pair_tokens[:, back * block : (back + 1) * block]

    outgoing = half_columns(1 - lane)
    theirs = send(outgoing, "pair")
    params = after(params, outgoing)
    momentum = after(momentum, outgoing)
    zero = jnp.zeros((), lane.dtype)
    pair_tokens = jnp.zeros((2 * rows, width // 2), inputs.dtype)
    pair_tokens = lax.dynamic_update_slice(
        pair_tokens, half_columns(lane), (lane * rows, zero)
    )
    pair_tokens = lax.dynamic_update_slice(pair_tokens, theirs, ((1 - lane) * rows, zero))
    pair_targets = lax.dynamic_update_slice(
        jnp.zeros((2 * rows, features), targets.dtype), targets[0], (lane * rows, zero)
    )
    replica = lax.axis_index("group")
    every = lax.all_gather(push_weight, "group", axis=0, tiled=True)
    weights = [push_weight]
    for step in range(STEPS):
        every = 0.5 * every + 0.5 * jnp.roll(every, 2**step)
        weights.append(lax.dynamic_slice_in_dim(every, replica, 1))
    kept = [[] for _ in range(STEPS)]
    passed = {}
    results = [jnp.zeros_like(params[0]), jnp.zeros_like(momentum[0])]

    def stream(c):
        state = chunk(params[0], c)
        moment = chunk(momentum[0], c)
        target = chunk(pair_targets, c).astype(wide)
        for step in range(STEPS):
            kept[step].append(state - (0.2 * 0.9) * moment)
            pieces = [(state / weights[step][0]).astype(narrow)]
            for _ in range(half - 1):
                pieces.append((yield pieces[-1], "line"))
            if step == 0:
                keys = jnp.dot(
                    pair_tokens, jnp.concatenate(pieces, axis=0), preferred_element_type=wide
                )
            else:
                keys = sum(
                    jnp.dot(column_block(back), piece, preferred_element_type=wide)
                    for back, piece in enumerate(pieces)
                )
            residual = key_scale * keys - target
            received = yield residual.astype(narrow), "pair"
            grad_out = (key_scale * (residual + received.astype(wide))).astype(narrow)

            def partial(back):
                return lax.dot_general(
                    column_block(back), grad_out, contract, preferred_element_type=wide
                )

            total = partial(1)
            for back in range(2, half + 1):
                arrived = yield total.astype(narrow), "line"
                total = arrived.astype(wide) + partial(back % half)
            behind = yield total.astype(narrow), "group"
            moment = 0.9 * moment + total
            mixed = 0.5 * (kept[step][c] + chunk(passed[step], c).astype(wide))
            state = mixed - 0.1 * (total + behind.astype(wide))
        fresh = [state / weights[STEPS][0], moment]
        for i in range(2):
            results[i] = lax.dynamic_update_slice(results[i], fresh[i], (0, c * part))
        yield None, None

    streams = [stream(c) for c in range(CHUNKS)]
    waiting = [next(running) for running in streams]
    groups_sent = [0] * CHUNKS
    for c in issue_order(half):
        value, link = waiting[c]
        result = send(value, link, 2 ** groups_sent[c])
        groups_sent[c] += link == "group"
        waiting[c] = streams[c].send(result)
        for step in range(STEPS):
            if step not in passed and len(kept[step]) == CHUNKS:
                if step == 0:
                    passed[step] = send(jnp.concatenate(kept[0], axis=1), "group", 1)
                else:
                    whole = jnp.concatenate(kept[step], axis=1).astype(narrow)
                    passed[step] = send(whole, "group", 2**step)
    return results[0][None], results[1][None]


def solution(mesh):
    return jax.shard_map(
        shards,
        mesh=mesh,
        in_specs=(
            P("group", "fsdp", None),
            P("group", "fsdp", None),
            P("group", "fsdp", None),
            P("group", "fsdp", None),
            P("group"),
        ),
        out_specs=(P("group", "fsdp", None), P("group", "fsdp", None)),
        check_vma=False,
    )
```

```python
import jax
import jax.numpy as jnp
from jax import lax
from jax.sharding import PartitionSpec as P

STEPS = 2
CHUNKS = 4
OCCUPANCY = {"gather": 2.75, "scatter": 2.75, "pair": 3.95, "group": 2.0}
PREPARE = {"gather": 0.8, "scatter": 1.2, "pair": 1.6, "group": 1.0}
LATENCY = 3.2


def from_behind(value, axis, steps):
    count = lax.axis_size(axis)
    pairs = [(source, (source + steps) % count) for source in range(count)]
    return lax.ppermute(value, axis, pairs)


def after(value, *earlier):
    return lax.optimization_barrier((value, *earlier))[0]


def issue_order(half):
    hops = half - 1
    plan = (["pair"] + ["scatter"] * hops + ["group"] + ["gather"] * hops) * STEPS
    plan = plan[: len(plan) - hops]
    free = dict.fromkeys(["line", "pair", "group", "core"], 0.0)
    ready = [2.0 * (c // 2) + 0.01 * c for c in range(CHUNKS)]
    at = [0] * CHUNKS
    order = []

    def due(c):
        idle = free["pair"] - OCCUPANCY["pair"] * (len(order) == 1)
        return max(ready[c], idle) if plan[at[c]] == "pair" else ready[c]

    while len(order) < CHUNKS * len(plan):
        c = min((c for c in range(CHUNKS) if at[c] < len(plan)), key=due)
        kind = plan[at[c]]
        link = kind if kind in free else "line"
        free["core"] = max(due(c), free["core"]) + PREPARE[kind]
        start = max(free["core"], free[link])
        free[link] = start + OCCUPANCY[kind]
        ready[c] = free[link] + LATENCY
        at[c] += 1
        order.append(c)
    return order


def shards(tokens, targets, params, momentum, push_weight):
    inputs = tokens[0]
    rows, width = inputs.shape
    features = params.shape[2]
    count = lax.axis_size("fsdp")
    half = count // 2
    block = width // count
    place = lax.div(lax.axis_index("fsdp"), 2)
    lane = lax.rem(lax.axis_index("fsdp"), 2)
    key_scale = width ** (-0.5)
    part = features // CHUNKS
    contract = (((0,), (0,)), ((), ()))
    wide = jnp.float32
    narrow = jnp.bfloat16
    issued = []

    def send(value, link, steps=1):
        if issued:
            value = after(value, issued[-1])
        issued.append(value)
        if link == "pair":
            return lax.ppermute(value, "fsdp", [(i, i ^ 1) for i in range(count)])
        if link == "line":
            return from_behind(value, "fsdp", 2)
        return from_behind(value, "group", steps)

    def chunk(array, c):
        return array[:, c * part : (c + 1) * part]

    def half_columns(source, side):
        pieces = []
        for back in range(half):
            start = (2 * lax.rem(place - back + half, half) + side) * block
            pieces.append(lax.dynamic_slice_in_dim(source, start, block, 1))
        return jnp.concatenate(pieces, axis=1)

    def column_block(back):
        return pair_tokens[:, back * block : (back + 1) * block]

    outgoing = half_columns(inputs, 1 - lane)
    theirs = send(outgoing, "pair")
    params = after(params, outgoing)
    momentum = after(momentum, outgoing)
    zero = jnp.zeros((), lane.dtype)
    pair_tokens = jnp.zeros((2 * rows, width // 2), inputs.dtype)
    pair_tokens = lax.dynamic_update_slice(
        pair_tokens, half_columns(after(inputs, outgoing), lane), (lane * rows, zero)
    )
    pair_tokens = lax.dynamic_update_slice(pair_tokens, theirs, ((1 - lane) * rows, zero))
    pair_targets = lax.dynamic_update_slice(
        jnp.zeros((2 * rows, features), targets.dtype), targets[0], (lane * rows, zero)
    )
    held = params.shape[1]
    results = [jnp.zeros_like(params[0]), jnp.zeros_like(momentum[0])]
    weights = [push_weight]
    kept, passed = [], []

    def debias(state, weight):
        return (state / weight[0]).astype(narrow)

    def exchange_kept(whole, step):
        kept.append(whole)
        if step == 0:
            extra = jnp.broadcast_to(weights[0], (8, features))
        else:
            left = weights[step]
            parts = []
            for _ in range(3):
                parts.append(lax.reduce_precision(left, 8, 7))
                left = left - parts[-1]
            row = lax.broadcasted_iota(jnp.int32, (16, features), 0)
            extra = jnp.where(row == 0, parts[0], jnp.where(row == 1, parts[1], parts[2]))
            whole, extra = whole.astype(narrow), extra.astype(narrow)
        got = send(jnp.concatenate([whole, extra], axis=0), "group", 2**step).astype(wide)
        passed.append(got[:held])
        came = got[held, :1] if step == 0 else jnp.sum(got[held : held + 3, :1], axis=0)
        weights.append(0.5 * weights[step] + 0.5 * came)

    first = [[debias(chunk(params[0], c), push_weight)] for c in range(CHUNKS)]
    for back in range(1, half):
        for c in range(CHUNKS):
            first[c].append(send(first[c][-1], "line"))
        if back == 1:
            exchange_kept(params[0] - (0.2 * 0.9) * momentum[0], 0)
    first_keys = []
    for c in range(0, CHUNKS, 2):
        both = [jnp.concatenate(first[i], axis=0) for i in (c, c + 1)]
        both = after(jnp.concatenate(both, axis=1), *first[c + 1][-1:])
        both = jnp.dot(pair_tokens, both, preferred_element_type=wide)
        first_keys += [both[:, :part], both[:, part:]]

    later = []

    def stream(c):
        moment = chunk(momentum[0], c)
        target = chunk(pair_targets, c).astype(wide)
        keys = first_keys[c]
        for step in range(STEPS):
            residual = key_scale * keys - target
            received = yield residual.astype(narrow), "pair"
            grad_out = (key_scale * (residual + received.astype(wide))).astype(narrow)

            def partial(back):
                return lax.dot_general(
                    column_block(back), grad_out, contract, preferred_element_type=wide
                )

            total = partial(1)
            for back in range(2, half + 1):
                arrived = yield total.astype(narrow), "line"
                total = arrived.astype(wide) + partial(back % half)
            behind = yield total.astype(narrow), "group"
            moment = 0.9 * moment + total
            mixed = 0.5 * (chunk(kept[step], c) + chunk(passed[step], c))
            state = mixed - 0.1 * (total + behind.astype(wide))
            if step == STEPS - 1:
                break
            later.append(state - (0.2 * 0.9) * moment)
            pieces = [debias(state, weights[step + 1])]
            for _ in range(half - 1):
                pieces.append((yield pieces[-1], "line"))
            keys = sum(
                jnp.dot(column_block(back), piece, preferred_element_type=wide)
                for back, piece in enumerate(pieces)
            )
        fresh = [state / weights[STEPS][0], moment]
        for i in range(2):
            results[i] = lax.dynamic_update_slice(results[i], fresh[i], (0, c * part))
        yield None, None

    streams = [stream(c) for c in range(CHUNKS)]
    came = [None] * CHUNKS
    mixings = [0] * CHUNKS
    for c in issue_order(half):
        came[c] = came[c] if came[c] is None else after(came[c], issued[-1])
        value, link = streams[c].send(came[c])
        came[c] = send(value, link, 2 ** mixings[c])
        mixings[c] += link == "group"
        if len(later) == CHUNKS:
            exchange_kept(jnp.concatenate(later, axis=1), mixings[c])
            later.clear()
    for c in range(CHUNKS):
        streams[c].send(came[c])
    return results[0][None], results[1][None]


def solution(mesh):
    return jax.shard_map(
        shards,
        mesh=mesh,
        in_specs=(
            P("group", "fsdp", None),
            P("group", "fsdp", None),
            P("group", "fsdp", None),
            P("group", "fsdp", None),
            P("group"),
        ),
        out_specs=(P("group", "fsdp", None), P("group", "fsdp", None)),
        check_vma=False,
    )
```

```python
import jax
import jax.numpy as jnp
from jax import lax
from jax.sharding import PartitionSpec as P

STEPS = 2
CHUNKS = 4
OCCUPANCY = {"gather": 2.75, "scatter": 2.75, "pair": 3.95, "group": 2.0}
PREPARE = {"gather": 0.8, "scatter": 1.2, "pair": 1.6, "group": 1.0}
LATENCY = 3.2


def from_behind(value, axis, steps):
    count = lax.axis_size(axis)
    pairs = [(source, (source + steps) % count) for source in range(count)]
    return lax.ppermute(value, axis, pairs)


def after(value, *earlier):
    return lax.optimization_barrier((value, *earlier))[0]


def issue_order(half):
    hops = half - 1
    plan = (["pair"] + ["scatter"] * hops + ["group"] + ["gather"] * hops) * STEPS
    plan = plan[: len(plan) - hops]
    free = dict.fromkeys(["line", "pair", "group", "core"], 0.0)
    ready = [2.0 * (c // 2) + 0.01 * c for c in range(CHUNKS)]
    at = [0] * CHUNKS
    order = []

    def due(c):
        idle = free["pair"] - OCCUPANCY["pair"] * (len(order) == 1)
        return max(ready[c], idle) if plan[at[c]] == "pair" else ready[c]

    while len(order) < CHUNKS * len(plan):
        c = min((c for c in range(CHUNKS) if at[c] < len(plan)), key=due)
        kind = plan[at[c]]
        link = kind if kind in free else "line"
        free["core"] = max(due(c), free["core"]) + PREPARE[kind]
        start = max(free["core"], free[link])
        free[link] = start + OCCUPANCY[kind]
        ready[c] = free[link] + LATENCY
        at[c] += 1
        order.append(c)
    return order


def shards(tokens, targets, params, momentum, push_weight):
    inputs = tokens[0]
    rows, width = inputs.shape
    features = params.shape[2]
    count = lax.axis_size("fsdp")
    half = count // 2
    block = width // count
    place = lax.div(lax.axis_index("fsdp"), 2)
    lane = lax.rem(lax.axis_index("fsdp"), 2)
    key_scale = width ** (-0.5)
    part = features // CHUNKS
    contract = (((0,), (0,)), ((), ()))
    wide = jnp.float32
    narrow = jnp.bfloat16
    issued = []

    def send(value, link, steps=1):
        if issued:
            value = after(value, issued[-1])
        issued.append(value)
        if link == "pair":
            return lax.ppermute(value, "fsdp", [(i, i ^ 1) for i in range(count)])
        if link == "line":
            return from_behind(value, "fsdp", 2)
        return from_behind(value, "group", steps)

    def chunk(array, c):
        return array[:, c * part : (c + 1) * part]

    def half_columns(source, side):
        pieces = []
        for back in range(half):
            start = (2 * lax.rem(place - back + half, half) + side) * block
            pieces.append(lax.dynamic_slice_in_dim(source, start, block, 1))
        return jnp.concatenate(pieces, axis=1)

    def column_block(back):
        return pair_tokens[:, back * block : (back + 1) * block]

    outgoing = half_columns(inputs, 1 - lane)
    theirs = lax.ppermute(outgoing, "fsdp", [(i, i ^ 1) for i in range(count)])
    params = after(params, outgoing)
    momentum = after(momentum, outgoing)
    zero = jnp.zeros((), lane.dtype)
    pair_tokens = jnp.zeros((2 * rows, width // 2), inputs.dtype)
    pair_tokens = lax.dynamic_update_slice(
        pair_tokens, half_columns(after(inputs, outgoing), lane), (lane * rows, zero)
    )
    pair_tokens = lax.dynamic_update_slice(pair_tokens, theirs, ((1 - lane) * rows, zero))
    pair_targets = lax.dynamic_update_slice(
        jnp.zeros((2 * rows, features), targets.dtype), targets[0], (lane * rows, zero)
    )
    held = params.shape[1]
    results = [jnp.zeros_like(params[0]), jnp.zeros_like(momentum[0])]
    weights = [push_weight]
    kept, passed = [], []

    def debias(state, weight):
        return (state / weight[0]).astype(narrow)

    def exchange_kept(whole, step):
        kept.append(whole)
        if step == 0:
            extra = jnp.broadcast_to(weights[0], (8, features))
        else:
            left = weights[step]
            parts = []
            for _ in range(3):
                parts.append(lax.reduce_precision(left, 8, 7))
                left = left - parts[-1]
            row = lax.broadcasted_iota(jnp.int32, (16, features), 0)
            extra = jnp.where(row == 0, parts[0], jnp.where(row == 1, parts[1], parts[2]))
            whole, extra = whole.astype(narrow), extra.astype(narrow)
        whole = jnp.concatenate([whole, extra], axis=0)
        passed.append(send(whole, "group", 2**step) if step else from_behind(whole, "group", 1))

    def read_passed(step):
        got = after(passed[step], issued[-1]).astype(wide)
        passed[step] = got[:held]
        came = got[held, :1] if step == 0 else jnp.sum(got[held : held + 3, :1], axis=0)
        weights.append(0.5 * weights[step] + 0.5 * came)

    first = [[debias(chunk(params[0], c), push_weight)] for c in range(CHUNKS)]
    for back in range(1, half):
        for c in range(CHUNKS):
            first[c].append(from_behind(first[c][-1], "fsdp", 2))
        if back == 1:
            exchange_kept(params[0] - (0.2 * 0.9) * momentum[0], 0)
    first_keys = []
    for c in range(0, CHUNKS, 2):
        both = [jnp.concatenate(first[i], axis=0) for i in (c, c + 1)]
        both = after(jnp.concatenate(both, axis=1))
        both = jnp.dot(pair_tokens, both, preferred_element_type=wide)
        first_keys += [both[:, :part], both[:, part:]]

    later = []

    def stream(c):
        moment = chunk(momentum[0], c)
        target = chunk(pair_targets, c).astype(wide)
        keys = first_keys[c]
        for step in range(STEPS):
            residual = key_scale * keys - target
            received = yield residual.astype(narrow), "pair"
            grad_out = (key_scale * (residual + received.astype(wide))).astype(narrow)

            def partial(back):
                return lax.dot_general(
                    column_block(back), grad_out, contract, preferred_element_type=wide
                )

            total = partial(1)
            for back in range(2, half + 1):
                arrived = yield total.astype(narrow), "line"
                if c == 0 and back == half:
                    read_passed(step)
                total = arrived.astype(wide) + partial(back % half)
            behind = yield total.astype(narrow), "group"
            moment = 0.9 * moment + total
            mixed = 0.5 * (chunk(kept[step], c) + chunk(passed[step], c))
            state = mixed - 0.1 * (total + behind.astype(wide))
            if step == STEPS - 1:
                break
            later.append(state - (0.2 * 0.9) * moment)
            pieces = [debias(state, weights[step + 1])]
            for _ in range(half - 1):
                pieces.append((yield pieces[-1], "line"))
            keys = sum(
                jnp.dot(column_block(back), piece, preferred_element_type=wide)
                for back, piece in enumerate(pieces)
            )
        fresh = [state / weights[STEPS][0], moment]
        for i in range(2):
            results[i] = lax.dynamic_update_slice(results[i], fresh[i], (0, c * part))
        yield None, None

    streams = [stream(c) for c in range(CHUNKS)]
    came = [None] * CHUNKS
    mixings = [0] * CHUNKS
    for c in issue_order(half):
        if came[c] is not None:
            came[c] = after(came[c], issued[-1])
        value, link = streams[c].send(came[c])
        came[c] = send(value, link, 2 ** mixings[c])
        mixings[c] += link == "group"
        if len(later) == CHUNKS:
            exchange_kept(jnp.concatenate(later, axis=1), mixings[c])
            later.clear()
    for c in range(CHUNKS):
        streams[c].send(came[c])
    return results[0][None], results[1][None]


def solution(mesh):
    return jax.shard_map(
        shards,
        mesh=mesh,
        in_specs=(
            P("group", "fsdp", None),
            P("group", "fsdp", None),
            P("group", "fsdp", None),
            P("group", "fsdp", None),
            P("group"),
        ),
        out_specs=(P("group", "fsdp", None), P("group", "fsdp", None)),
        check_vma=False,
    )
```

```python
import jax
import jax.numpy as jnp
from jax import lax
from jax.sharding import PartitionSpec as P

STEPS = 2
CHUNKS = 4
OCCUPANCY = {"gather": 2.75, "scatter": 2.75, "pair": 3.95, "group": 2.0}
PREPARE = {"gather": 0.8, "scatter": 1.2, "pair": 1.6, "group": 1.0}
LATENCY = 3.2


def from_behind(value, axis, steps):
    count = lax.axis_size(axis)
    pairs = [(source, (source + steps) % count) for source in range(count)]
    return lax.ppermute(value, axis, pairs)


def after(value, *earlier):
    return lax.optimization_barrier((value, *earlier))[0]


def issue_order(half):
    hops = half - 1
    plan = (["pair"] + ["scatter"] * hops + ["group"] + ["gather"] * hops) * STEPS
    plan = plan[: len(plan) - hops]
    free = dict.fromkeys(["line", "pair", "group", "core"], 0.0)
    ready = [2.0 * (c // 2) + 0.01 * c for c in range(CHUNKS)]
    at = [0] * CHUNKS
    order = []

    def due(c):
        idle = free["pair"] - OCCUPANCY["pair"] * (len(order) == 1)
        return max(ready[c], idle) if plan[at[c]] == "pair" else ready[c]

    while len(order) < CHUNKS * len(plan):
        c = min((c for c in range(CHUNKS) if at[c] < len(plan)), key=due)
        kind = plan[at[c]]
        link = kind if kind in free else "line"
        free["core"] = max(due(c), free["core"]) + PREPARE[kind]
        start = max(free["core"], free[link])
        free[link] = start + OCCUPANCY[kind]
        ready[c] = free[link] + LATENCY
        at[c] += 1
        order.append(c)
    return order


def shards(tokens, targets, params, momentum, push_weight):
    inputs = tokens[0]
    rows, width = inputs.shape
    features = params.shape[2]
    count = lax.axis_size("fsdp")
    half = count // 2
    block = width // count
    place = lax.div(lax.axis_index("fsdp"), 2)
    lane = lax.rem(lax.axis_index("fsdp"), 2)
    key_scale = width ** (-0.5)
    part = features // CHUNKS
    contract = (((0,), (0,)), ((), ()))
    wide = jnp.float32
    narrow = jnp.bfloat16
    issued = []

    def send(value, link, steps=1):
        if issued:
            value = after(value, issued[-1])
        issued.append(value)
        if link == "pair":
            return lax.ppermute(value, "fsdp", [(i, i ^ 1) for i in range(count)])
        if link == "line":
            return from_behind(value, "fsdp", 2)
        return from_behind(value, "group", steps)

    def chunk(array, c):
        return array[:, c * part : (c + 1) * part]

    def half_columns(source, side):
        pieces = []
        for back in range(half):
            start = (2 * lax.rem(place - back + half, half) + side) * block
            pieces.append(lax.dynamic_slice_in_dim(source, start, block, 1))
        return jnp.concatenate(pieces, axis=1)

    def column_block(back):
        return pair_tokens[:, back * block : (back + 1) * block]

    outgoing = half_columns(inputs, 1 - lane)
    theirs = lax.ppermute(outgoing, "fsdp", [(i, i ^ 1) for i in range(count)])
    params = after(params, outgoing)
    momentum = after(momentum, outgoing)
    zero = jnp.zeros((), lane.dtype)
    pair_tokens = jnp.zeros((2 * rows, width // 2), inputs.dtype)
    pair_tokens = lax.dynamic_update_slice(
        pair_tokens, half_columns(after(inputs, outgoing), lane), (lane * rows, zero)
    )
    pair_tokens = lax.dynamic_update_slice(pair_tokens, theirs, ((1 - lane) * rows, zero))
    pair_targets = lax.dynamic_update_slice(
        jnp.zeros((2 * rows, features), targets.dtype), targets[0], (lane * rows, zero)
    )
    held = params.shape[1]
    results = [jnp.zeros_like(params[0]), jnp.zeros_like(momentum[0])]
    weights = [jnp.broadcast_to(push_weight, (1, features))]
    kept, passed = [], []

    def debias(state, weight):
        return (state / weight).astype(narrow)

    def exchange_kept(whole, step):
        kept.append(whole)
        if step == 0:
            extra = jnp.broadcast_to(weights[0], (8, features))
        else:
            left = jnp.broadcast_to(weights[step], (16, features))
            parts = []
            for _ in range(3):
                parts.append(lax.reduce_precision(left, 8, 7))
                left = left - parts[-1]
            row = lax.broadcasted_iota(jnp.int32, (16, features), 0)
            extra = jnp.where(row == 0, parts[0], jnp.where(row == 1, parts[1], parts[2]))
            whole, extra = whole.astype(narrow), extra.astype(narrow)
        whole = jnp.concatenate([whole, extra], axis=0)
        passed.append(send(whole, "group", 2**step) if step else from_behind(whole, "group", 1))

    def read_passed(step):
        got = after(passed[step], issued[-1]).astype(wide)
        passed[step] = got[:held]
        came = got[held : held + 1]
        if step > 0:
            came = came + got[held + 1 : held + 2] + got[held + 2 : held + 3]
        weights.append(0.5 * weights[step] + 0.5 * came)

    first = [[debias(chunk(params[0], c), push_weight[0])] for c in range(CHUNKS)]
    for back in range(1, half):
        for c in range(CHUNKS):
            first[c].append(from_behind(first[c][-1], "fsdp", 2))
        if back == 1:
            exchange_kept(params[0] - (0.2 * 0.9) * momentum[0], 0)
    first_keys = []
    for c in range(0, CHUNKS, 2):
        both = [jnp.concatenate(first[i], axis=0) for i in (c, c + 1)]
        both = after(jnp.concatenate(both, axis=1))
        both = jnp.dot(pair_tokens, both, preferred_element_type=wide)
        first_keys += [both[:, :part], both[:, part:]]

    later = []

    def stream(c):
        moment = chunk(momentum[0], c)
        target = chunk(pair_targets, c).astype(wide)
        keys = first_keys[c]
        for step in range(STEPS):
            residual = key_scale * keys - target
            received = yield residual.astype(narrow), "pair"
            grad_out = (key_scale * (residual + received.astype(wide))).astype(narrow)

            def partial(back):
                return lax.dot_general(
                    column_block(back), grad_out, contract, preferred_element_type=wide
                )

            total = partial(1)
            for back in range(2, half + 1):
                arrived = yield total.astype(narrow), "line"
                if step > 0 and c == 0 and back == half:
                    read_passed(step)
                total = arrived.astype(wide) + partial(back % half)
            behind = yield total.astype(narrow), "group"
            moment = 0.9 * moment + total
            mixed = 0.5 * (chunk(kept[step], c) + chunk(passed[step], c))
            state = mixed - 0.1 * (total + behind.astype(wide))
            if step == STEPS - 1:
                break
            later.append(state - (0.2 * 0.9) * moment)
            pieces = [debias(state, chunk(weights[step + 1], c))]
            for _ in range(half - 1):
                pieces.append((yield pieces[-1], "line"))
            keys = sum(
                jnp.dot(column_block(back), piece, preferred_element_type=wide)
                for back, piece in enumerate(pieces)
            )
        fresh = [state / chunk(weights[STEPS], c), moment]
        for i in range(2):
            results[i] = lax.dynamic_update_slice(results[i], fresh[i], (0, c * part))
        yield None, None

    streams = [stream(c) for c in range(CHUNKS)]
    came = [None] * CHUNKS
    mixings = [0] * CHUNKS
    for c in issue_order(half):
        if came[c] is not None:
            came[c] = after(came[c], issued[-1])
        value, link = streams[c].send(came[c])
        came[c] = send(value, link, 2 ** mixings[c])
        if len(issued) == 2:
            read_passed(0)
            issued.append(weights[1])
        mixings[c] += link == "group"
        if len(later) == CHUNKS:
            exchange_kept(jnp.concatenate(later, axis=1), mixings[c])
            later.clear()
    for c in range(CHUNKS):
        streams[c].send(came[c])
    return results[0][None], results[1][None]


def solution(mesh):
    return jax.shard_map(
        shards,
        mesh=mesh,
        in_specs=(
            P("group", "fsdp", None),
            P("group", "fsdp", None),
            P("group", "fsdp", None),
            P("group", "fsdp", None),
            P("group"),
        ),
        out_specs=(P("group", "fsdp", None), P("group", "fsdp", None)),
        check_vma=False,
    )
```

```python
import jax
import jax.numpy as jnp
from jax import lax
from jax.sharding import PartitionSpec as P

STEPS = 2
CHUNKS = 4
OCCUPANCY = {"gather": 2.75, "scatter": 2.75, "pair": 3.95, "group": 2.0}
PREPARE = {"gather": 0.8, "scatter": 1.2, "pair": 1.6, "group": 1.0}
LATENCY = 3.2


def from_behind(value, axis, steps):
    count = lax.axis_size(axis)
    pairs = [(source, (source + steps) % count) for source in range(count)]
    return lax.ppermute(value, axis, pairs)


def after(value, *earlier):
    return lax.optimization_barrier((value, *earlier))[0]


def issue_order(half):
    hops = half - 1
    plan = (["pair"] + ["scatter"] * hops + ["group"] + ["gather"] * hops) * STEPS
    plan = plan[: len(plan) - hops]
    free = dict.fromkeys(["line", "pair", "group", "core"], 0.0)
    ready = [2.0 * (c // 2) + 0.01 * c for c in range(CHUNKS)]
    at = [0] * CHUNKS
    order = []

    def due(c):
        idle = free["pair"] - OCCUPANCY["pair"] * (len(order) == 1)
        return max(ready[c], idle) if plan[at[c]] == "pair" else ready[c]

    while len(order) < CHUNKS * len(plan):
        c = min((c for c in range(CHUNKS) if at[c] < len(plan)), key=due)
        kind = plan[at[c]]
        link = kind if kind in free else "line"
        free["core"] = max(due(c), free["core"]) + PREPARE[kind]
        start = max(free["core"], free[link])
        free[link] = start + OCCUPANCY[kind]
        ready[c] = free[link] + LATENCY
        at[c] += 1
        order.append(c)
    return order


def shards(tokens, targets, params, momentum, push_weight):
    inputs = tokens[0]
    rows, width = inputs.shape
    features = params.shape[2]
    count = lax.axis_size("fsdp")
    half = count // 2
    block = width // count
    place = lax.div(lax.axis_index("fsdp"), 2)
    lane = lax.rem(lax.axis_index("fsdp"), 2)
    key_scale = width ** (-0.5)
    part = features // CHUNKS
    contract = (((0,), (0,)), ((), ()))
    wide = jnp.float32
    narrow = jnp.bfloat16
    issued = []

    def send(value, link, steps=1):
        if issued:
            value = after(value, issued[-1])
        issued.append(value)
        if link == "pair":
            return lax.ppermute(value, "fsdp", [(i, i ^ 1) for i in range(count)])
        if link == "line":
            return from_behind(value, "fsdp", 2)
        return from_behind(value, "group", steps)

    def chunk(array, c):
        return array[:, c * part : (c + 1) * part]

    def half_columns(source, side):
        pieces = []
        for back in range(half):
            start = (2 * lax.rem(place - back + half, half) + side) * block
            pieces.append(lax.dynamic_slice_in_dim(source, start, block, 1))
        return jnp.concatenate(pieces, axis=1)

    def column_block(back):
        return pair_tokens[:, back * block : (back + 1) * block]

    outgoing = half_columns(inputs, 1 - lane)
    theirs = lax.ppermute(outgoing, "fsdp", [(i, i ^ 1) for i in range(count)])
    params = after(params, outgoing)
    momentum = after(momentum, outgoing)
    zero = jnp.zeros((), lane.dtype)
    pair_tokens = jnp.zeros((2 * rows, width // 2), inputs.dtype)
    pair_tokens = lax.dynamic_update_slice(
        pair_tokens, half_columns(after(inputs, outgoing), lane), (lane * rows, zero)
    )
    pair_tokens = lax.dynamic_update_slice(pair_tokens, theirs, ((1 - lane) * rows, zero))
    pair_targets = lax.dynamic_update_slice(
        jnp.zeros((2 * rows, features), targets.dtype), targets[0], (lane * rows, zero)
    )
    held = params.shape[1]
    results = [jnp.zeros_like(params[0]), jnp.zeros_like(momentum[0])]
    weights = [jnp.broadcast_to(push_weight, (1, features))]
    kept, passed = [], []

    def debias(state, weight):
        return (state / weight).astype(narrow)

    def exchange_kept(whole, step):
        kept.append(whole)
        if step == 0:
            extra = jnp.broadcast_to(weights[0], (8, features))
        else:
            left = jnp.broadcast_to(weights[step], (16, features))
            parts = []
            for _ in range(3):
                parts.append(lax.reduce_precision(left, 8, 7))
                left = left - parts[-1]
            row = lax.broadcasted_iota(jnp.int32, (16, features), 0)
            extra = jnp.where(row == 0, parts[0], jnp.where(row == 1, parts[1], parts[2]))
            whole, extra = whole.astype(narrow), extra.astype(narrow)
        whole = jnp.concatenate([whole, extra], axis=0)
        passed.append(send(whole, "group", 2**step) if step else from_behind(whole, "group", 1))

    def read_passed(step):
        got = after(passed[step], issued[-1]).astype(wide)
        passed[step] = got[:held]
        came = got[held : held + 1]
        if step > 0:
            came = came + got[held + 1 : held + 2] + got[held + 2 : held + 3]
        weights.append(0.5 * weights[step] + 0.5 * came)

    first = [[debias(chunk(params[0], c), push_weight[0])] for c in range(CHUNKS)]
    for back in range(1, half):
        for c in range(CHUNKS):
            first[c].append(from_behind(first[c][-1], "fsdp", 2))
        if back == 1:
            exchange_kept(params[0] - (0.2 * 0.9) * momentum[0], 0)
    first_keys = []

    def multiply_first():
        c = len(first_keys)
        both = []
        for pieces in first[c : c + 2]:
            last = after(pieces[-1], issued[-1]) if issued else pieces[-1]
            both.append(jnp.concatenate(pieces[:-1] + [last], axis=0))
        both = after(jnp.concatenate(both, axis=1))
        both = jnp.dot(pair_tokens, both, preferred_element_type=wide)
        first_keys.extend([both[:, :part], both[:, part:]])

    multiply_first()
    later = []

    def stream(c):
        moment = chunk(momentum[0], c)
        target = chunk(pair_targets, c).astype(wide)
        keys = first_keys[c]
        for step in range(STEPS):
            residual = key_scale * keys - target
            received = yield residual.astype(narrow), "pair"
            grad_out = (key_scale * (residual + received.astype(wide))).astype(narrow)

            def partial(back):
                return lax.dot_general(
                    column_block(back), grad_out, contract, preferred_element_type=wide
                )

            total = partial(1)
            for back in range(2, half + 1):
                arrived = yield total.astype(narrow), "line"
                if step > 0 and c == 0 and back == half:
                    read_passed(step)
                total = arrived.astype(wide) + partial(back % half)
            behind = yield total.astype(narrow), "group"
            moment = 0.9 * moment + total
            mixed = 0.5 * (chunk(kept[step], c) + chunk(passed[step], c))
            state = mixed - 0.1 * (total + behind.astype(wide))
            if step == STEPS - 1:
                break
            later.append(state - (0.2 * 0.9) * moment)
            pieces = [debias(state, chunk(weights[step + 1], c))]
            for _ in range(half - 1):
                pieces.append((yield pieces[-1], "line"))
            keys = sum(
                jnp.dot(column_block(back), piece, preferred_element_type=wide)
                for back, piece in enumerate(pieces)
            )
        fresh = [state / chunk(weights[STEPS], c), moment]
        for i in range(2):
            results[i] = lax.dynamic_update_slice(results[i], fresh[i], (0, c * part))
        yield None, None

    streams = [stream(c) for c in range(CHUNKS)]
    came = [None] * CHUNKS
    mixings = [0] * CHUNKS
    for c in issue_order(half):
        if came[c] is not None:
            came[c] = after(came[c], issued[-1])
        value, link = streams[c].send(came[c])
        came[c] = send(value, link, 2 ** mixings[c])
        if len(issued) == 2:
            while len(first_keys) < CHUNKS:
                multiply_first()
            read_passed(0)
            issued.append(weights[1])
        mixings[c] += link == "group"
        if len(later) == CHUNKS:
            exchange_kept(jnp.concatenate(later, axis=1), mixings[c])
            later.clear()
    for c in range(CHUNKS):
        streams[c].send(came[c])
    return results[0][None], results[1][None]


def solution(mesh):
    return jax.shard_map(
        shards,
        mesh=mesh,
        in_specs=(
            P("group", "fsdp", None),
            P("group", "fsdp", None),
            P("group", "fsdp", None),
            P("group", "fsdp", None),
            P("group"),
        ),
        out_specs=(P("group", "fsdp", None), P("group", "fsdp", None)),
        check_vma=False,
    )
```

```python
import jax
import jax.numpy as jnp
from jax import lax
from jax.sharding import PartitionSpec as P

STEPS = 2
CHUNKS = 4
OCCUPANCY = {"gather": 2.75, "scatter": 2.75, "pair": 3.95, "group": 2.0}
PREPARE = {"gather": 1.4, "scatter": 1.8, "pair": 2.6, "group": 2.2}
LATENCY = 3.2


def from_behind(value, axis, steps):
    count = lax.axis_size(axis)
    pairs = [(source, (source + steps) % count) for source in range(count)]
    return lax.ppermute(value, axis, pairs)


def after(value, *earlier):
    return lax.optimization_barrier((value, *earlier))[0]


def issue_order(half):
    hops = half - 1
    plan = (["pair"] + ["scatter"] * hops + ["group"] + ["gather"] * hops) * STEPS
    plan = plan[: len(plan) - hops]
    free = dict.fromkeys(["line", "pair", "group", "core"], 0.0)
    ready = [2.0 * (c // 2) + 0.01 * c for c in range(CHUNKS)]
    at = [0] * CHUNKS
    order = []

    def due(c):
        idle = free["pair"] - OCCUPANCY["pair"] * (len(order) == 1)
        return max(ready[c], idle) if plan[at[c]] == "pair" else ready[c]

    while len(order) < CHUNKS * len(plan):
        c = min((c for c in range(CHUNKS) if at[c] < len(plan)), key=due)
        kind = plan[at[c]]
        link = kind if kind in free else "line"
        free["core"] = max(due(c), free["core"]) + PREPARE[kind]
        start = max(free["core"], free[link])
        free[link] = start + OCCUPANCY[kind]
        ready[c] = free[link] + LATENCY
        at[c] += 1
        order.append(c)
    return order


def shards(tokens, targets, params, momentum, push_weight):
    inputs = tokens[0]
    rows, width = inputs.shape
    features = params.shape[2]
    count = lax.axis_size("fsdp")
    half = count // 2
    block = width // count
    place = lax.div(lax.axis_index("fsdp"), 2)
    lane = lax.rem(lax.axis_index("fsdp"), 2)
    key_scale = width ** (-0.5)
    part = features // CHUNKS
    contract = (((0,), (0,)), ((), ()))
    wide = jnp.float32
    narrow = jnp.bfloat16
    issued = []

    def send(value, link, steps=1):
        if issued:
            value = after(value, issued[-1])
        issued.append(value)
        if link == "pair":
            return lax.ppermute(value, "fsdp", [(i, i ^ 1) for i in range(count)])
        if link == "line":
            return from_behind(value, "fsdp", 2)
        return from_behind(value, "group", steps)

    def chunk(array, c):
        return array[:, c * part : (c + 1) * part]

    def half_columns(source, side):
        pieces = []
        for back in range(half):
            start = (2 * lax.rem(place - back + half, half) + side) * block
            pieces.append(lax.dynamic_slice_in_dim(source, start, block, 1))
        return jnp.concatenate(pieces, axis=1)

    def column_block(back):
        return pair_tokens[:, back * block : (back + 1) * block]

    outgoing = half_columns(inputs, 1 - lane)
    theirs = lax.ppermute(outgoing, "fsdp", [(i, i ^ 1) for i in range(count)])
    params = after(params, outgoing)
    momentum = after(momentum, outgoing)
    zero = jnp.zeros((), lane.dtype)
    pair_tokens = jnp.zeros((2 * rows, width // 2), inputs.dtype)
    pair_tokens = lax.dynamic_update_slice(
        pair_tokens, half_columns(after(inputs, outgoing), lane), (lane * rows, zero)
    )
    pair_tokens = lax.dynamic_update_slice(pair_tokens, theirs, ((1 - lane) * rows, zero))
    pair_targets = lax.dynamic_update_slice(
        jnp.zeros((2 * rows, features), targets.dtype), targets[0], (lane * rows, zero)
    )
    held = params.shape[1]
    results = [jnp.zeros_like(params[0]), jnp.zeros_like(momentum[0])]
    weights = [jnp.broadcast_to(push_weight, (1, features))]
    kept, passed = [], []

    def debias(state, weight):
        return (state / weight).astype(narrow)

    def exchange_kept(whole, step):
        kept.append(whole)
        if step == 0:
            extra = jnp.broadcast_to(weights[0], (8, features))
        else:
            left = jnp.broadcast_to(weights[step], (16, features))
            parts = []
            for _ in range(3):
                parts.append(lax.reduce_precision(left, 8, 7))
                left = left - parts[-1]
            row = lax.broadcasted_iota(jnp.int32, (16, features), 0)
            extra = jnp.where(row == 0, parts[0], jnp.where(row == 1, parts[1], parts[2]))
            whole, extra = whole.astype(narrow), extra.astype(narrow)
        whole = jnp.concatenate([whole, extra], axis=0)
        passed.append(send(whole, "group", 2**step) if step else from_behind(whole, "group", 1))

    def read_passed(step):
        got = after(passed[step], issued[-1]).astype(wide)
        passed[step] = got[:held]
        came = got[held : held + 1]
        if step > 0:
            came = came + got[held + 1 : held + 2] + got[held + 2 : held + 3]
        weights.append(0.5 * weights[step] + 0.5 * came)

    first = [[debias(chunk(params[0], c), push_weight[0])] for c in range(CHUNKS)]
    for back in range(1, half):
        for c in range(CHUNKS):
            first[c].append(from_behind(first[c][-1], "fsdp", 2))
        if back == 1:
            exchange_kept(params[0] - (0.2 * 0.9) * momentum[0], 0)
    first_keys = []

    def multiply_first():
        c = len(first_keys)
        both = []
        for pieces in first[c : c + 2]:
            last = after(pieces[-1], issued[-1]) if issued else pieces[-1]
            both.append(jnp.concatenate(pieces[:-1] + [last], axis=0))
        both = after(jnp.concatenate(both, axis=1))
        both = jnp.dot(pair_tokens, both, preferred_element_type=wide)
        first_keys.extend([both[:, :part], both[:, part:]])

    multiply_first()
    later = []

    def stream(c):
        moment = chunk(momentum[0], c)
        target = chunk(pair_targets, c).astype(wide)
        keys = first_keys[c]
        for step in range(STEPS):
            residual = key_scale * keys - target
            received = yield residual.astype(narrow), "pair"
            grad_out = (key_scale * (residual + received.astype(wide))).astype(narrow)

            def partial(back):
                return lax.dot_general(
                    column_block(back), grad_out, contract, preferred_element_type=wide
                )

            total = partial(1)
            for back in range(2, half + 1):
                arrived = yield total.astype(narrow), "line"
                if step > 0 and c == 0 and back == half:
                    read_passed(step)
                total = arrived.astype(wide) + partial(back % half)
            behind = yield total.astype(narrow), "group"
            moment = 0.9 * moment + total
            mixed = 0.5 * (chunk(kept[step], c) + chunk(passed[step], c))
            state = mixed - 0.1 * (total + behind.astype(wide))
            if step == STEPS - 1:
                break
            later.append(state - (0.2 * 0.9) * moment)
            pieces = [debias(state, chunk(weights[step + 1], c))]
            for _ in range(half - 1):
                pieces.append((yield pieces[-1], "line"))
            keys = sum(
                jnp.dot(column_block(back), piece, preferred_element_type=wide)
                for back, piece in enumerate(pieces)
            )
        fresh = [state / chunk(weights[STEPS], c), moment]
        for i in range(2):
            results[i] = lax.dynamic_update_slice(results[i], fresh[i], (0, c * part))
        yield None, None

    streams = [stream(c) for c in range(CHUNKS)]
    came = [None] * CHUNKS
    mixings = [0] * CHUNKS
    for c in issue_order(half):
        if came[c] is not None:
            came[c] = after(came[c], issued[-1])
        value, link = streams[c].send(came[c])
        came[c] = send(value, link, 2 ** mixings[c])
        if len(issued) == 2:
            while len(first_keys) < CHUNKS:
                multiply_first()
            read_passed(0)
            issued.append(weights[1])
        mixings[c] += link == "group"
        if len(later) == CHUNKS:
            exchange_kept(jnp.concatenate(later, axis=1), mixings[c])
            later.clear()
    for c in range(CHUNKS):
        streams[c].send(came[c])
    return results[0][None], results[1][None]


def solution(mesh):
    return jax.shard_map(
        shards,
        mesh=mesh,
        in_specs=(
            P("group", "fsdp", None),
            P("group", "fsdp", None),
            P("group", "fsdp", None),
            P("group", "fsdp", None),
            P("group"),
        ),
        out_specs=(P("group", "fsdp", None), P("group", "fsdp", None)),
        check_vma=False,
    )
```

```python
import jax
import jax.numpy as jnp
from jax import lax
from jax.sharding import PartitionSpec as P

STEPS = 2
CHUNKS = 4
OCCUPANCY = {"gather": 2.75, "scatter": 2.75, "pair": 3.95, "group": 2.0}
PREPARE = {"gather": 1.4, "scatter": 1.8, "pair": 2.6, "group": 2.2}
LATENCY = 3.2


def from_behind(value, axis, steps):
    count = lax.axis_size(axis)
    pairs = [(source, (source + steps) % count) for source in range(count)]
    return lax.ppermute(value, axis, pairs)


def after(value, *earlier):
    return lax.optimization_barrier((value, *earlier))[0]


def issue_order(half):
    hops = half - 1
    plan = (["pair"] + ["scatter"] * hops + ["group"] + ["gather"] * hops) * STEPS
    plan = plan[: len(plan) - hops]
    free = dict.fromkeys(["line", "pair", "group", "core"], 0.0)
    ready = [2.0 * (c // 2) + 0.01 * c for c in range(CHUNKS)]
    at = [0] * CHUNKS
    order = []

    def due(c):
        idle = free["pair"] - OCCUPANCY["pair"] * (len(order) == 1)
        return max(ready[c], idle) if plan[at[c]] == "pair" else ready[c]

    while len(order) < CHUNKS * len(plan):
        c = min((c for c in range(CHUNKS) if at[c] < len(plan)), key=due)
        kind = plan[at[c]]
        link = kind if kind in free else "line"
        free["core"] = max(due(c), free["core"]) + PREPARE[kind]
        start = max(free["core"], free[link])
        free[link] = start + OCCUPANCY[kind]
        ready[c] = free[link] + LATENCY
        at[c] += 1
        order.append(c)
    return order


def shards(tokens, targets, params, momentum, push_weight):
    inputs = tokens[0]
    rows, width = inputs.shape
    features = params.shape[2]
    count = lax.axis_size("fsdp")
    half = count // 2
    block = width // count
    place = lax.div(lax.axis_index("fsdp"), 2)
    lane = lax.rem(lax.axis_index("fsdp"), 2)
    key_scale = width ** (-0.5)
    part = features // CHUNKS
    contract = (((0,), (0,)), ((), ()))
    wide = jnp.float32
    narrow = jnp.bfloat16
    issued = []

    def send(value, link, steps=1):
        if issued:
            value = after(value, issued[-1])
        issued.append(value)
        if link == "pair":
            return lax.ppermute(value, "fsdp", [(i, i ^ 1) for i in range(count)])
        if link == "line":
            return from_behind(value, "fsdp", 2)
        return from_behind(value, "group", steps)

    def chunk(array, c):
        return array[:, c * part : (c + 1) * part]

    def half_columns(source, side):
        pieces = []
        for back in range(half):
            start = (2 * lax.rem(place - back + half, half) + side) * block
            pieces.append(lax.dynamic_slice_in_dim(source, start, block, 1))
        return jnp.concatenate(pieces, axis=1)

    def column_block(back):
        return joined[0][:, back * block : (back + 1) * block]

    outgoing = half_columns(inputs, 1 - lane)
    theirs = lax.ppermute(outgoing, "fsdp", [(i, i ^ 1) for i in range(count)])
    params = after(params, outgoing)
    momentum = after(momentum, outgoing)
    zero = jnp.zeros((), lane.dtype)
    mine = half_columns(after(inputs, outgoing), lane)

    def in_lane_order(own, other):
        both = jnp.zeros((2 * rows, own.shape[1]), own.dtype)
        both = lax.dynamic_update_slice(both, own, (lane * rows, zero))
        return lax.dynamic_update_slice(both, other, ((1 - lane) * rows, zero))

    joined = []
    pair_targets = lax.dynamic_update_slice(
        jnp.zeros((2 * rows, features), targets.dtype), targets[0], (lane * rows, zero)
    )
    held = params.shape[1]
    results = [jnp.zeros_like(params[0]), jnp.zeros_like(momentum[0])]
    weights = [jnp.broadcast_to(push_weight, (1, features))]
    kept, passed = [], []

    def debias(state, weight):
        return (state / weight).astype(narrow)

    def exchange_kept(whole, step):
        kept.append(whole)
        if step == 0:
            extra = jnp.broadcast_to(weights[0], (8, features))
        else:
            left = jnp.broadcast_to(weights[step], (16, features))
            parts = []
            for _ in range(3):
                parts.append(lax.reduce_precision(left, 8, 7))
                left = left - parts[-1]
            row = lax.broadcasted_iota(jnp.int32, (16, features), 0)
            extra = jnp.where(row == 0, parts[0], jnp.where(row == 1, parts[1], parts[2]))
            whole, extra = whole.astype(narrow), extra.astype(narrow)
        whole = jnp.concatenate([whole, extra], axis=0)
        passed.append(send(whole, "group", 2**step) if step else from_behind(whole, "group", 1))

    def read_passed(step):
        got = after(passed[step], issued[-1]).astype(wide)
        passed[step] = got[:held]
        came = got[held : held + 1]
        if step > 0:
            came = came + got[held + 1 : held + 2] + got[held + 2 : held + 3]
        weights.append(0.5 * weights[step] + 0.5 * came)

    first = [[debias(chunk(params[0], c), push_weight[0])] for c in range(CHUNKS)]
    for back in range(1, half):
        for c in range(CHUNKS):
            first[c].append(from_behind(first[c][-1], "fsdp", 2))
        if back == 1:
            exchange_kept(params[0] - (0.2 * 0.9) * momentum[0], 0)
    first_keys = []

    def multiply_first():
        c = len(first_keys)
        both = []
        for pieces in first[c : c + 2]:
            last = after(pieces[-1], issued[-1]) if issued else pieces[-1]
            both.append(jnp.concatenate(pieces[:-1] + [last], axis=0))
        both = after(jnp.concatenate(both, axis=1))
        if joined:
            both = jnp.dot(joined[0], both, preferred_element_type=wide)
        else:
            both = in_lane_order(
                jnp.dot(mine, both, preferred_element_type=wide),
                jnp.dot(theirs, both, preferred_element_type=wide),
            )
        first_keys.extend([both[:, :part], both[:, part:]])

    multiply_first()
    later = []

    def stream(c):
        moment = chunk(momentum[0], c)
        target = chunk(pair_targets, c).astype(wide)
        keys = first_keys[c]
        for step in range(STEPS):
            residual = key_scale * keys - target
            received = yield residual.astype(narrow), "pair"
            grad_out = (key_scale * (residual + received.astype(wide))).astype(narrow)

            def partial(back):
                return lax.dot_general(
                    column_block(back), grad_out, contract, preferred_element_type=wide
                )

            total = partial(1)
            for back in range(2, half + 1):
                arrived = yield total.astype(narrow), "line"
                if step > 0 and c == 0 and back == half:
                    read_passed(step)
                total = arrived.astype(wide) + partial(back % half)
            behind = yield total.astype(narrow), "group"
            moment = 0.9 * moment + total
            mixed = 0.5 * (chunk(kept[step], c) + chunk(passed[step], c))
            state = mixed - 0.1 * (total + behind.astype(wide))
            if step == STEPS - 1:
                break
            later.append(state - (0.2 * 0.9) * moment)
            pieces = [debias(state, chunk(weights[step + 1], c))]
            for _ in range(half - 1):
                pieces.append((yield pieces[-1], "line"))
            keys = sum(
                jnp.dot(column_block(back), piece, preferred_element_type=wide)
                for back, piece in enumerate(pieces)
            )
        fresh = [state / chunk(weights[STEPS], c), moment]
        for i in range(2):
            results[i] = lax.dynamic_update_slice(results[i], fresh[i], (0, c * part))
        yield None, None

    streams = [stream(c) for c in range(CHUNKS)]
    came = [None] * CHUNKS
    mixings = [0] * CHUNKS
    for c in issue_order(half):
        if came[c] is not None:
            came[c] = after(came[c], issued[-1])
        value, link = streams[c].send(came[c])
        came[c] = send(value, link, 2 ** mixings[c])
        if len(issued) == 2:
            joined.append(in_lane_order(mine, after(theirs, issued[-1])))
            while len(first_keys) < CHUNKS:
                multiply_first()
            read_passed(0)
            issued.append(weights[1])
        mixings[c] += link == "group"
        if len(later) == CHUNKS:
            exchange_kept(jnp.concatenate(later, axis=1), mixings[c])
            later.clear()
    for c in range(CHUNKS):
        streams[c].send(came[c])
    return results[0][None], results[1][None]


def solution(mesh):
    return jax.shard_map(
        shards,
        mesh=mesh,
        in_specs=(
            P("group", "fsdp", None),
            P("group", "fsdp", None),
            P("group", "fsdp", None),
            P("group", "fsdp", None),
            P("group"),
        ),
        out_specs=(P("group", "fsdp", None), P("group", "fsdp", None)),
        check_vma=False,
    )
```

```python
import jax
import jax.numpy as jnp
from jax import lax
from jax.sharding import PartitionSpec as P

STEPS = 2
CHUNKS = 4
OCCUPANCY = {"gather": 2.75, "scatter": 2.75, "pair": 3.95, "group": 2.0}
PREPARE = {"gather": 1.4, "scatter": 1.8, "pair": 2.6, "group": 2.2}
LATENCY = 4.2


def from_behind(value, axis, steps):
    count = lax.axis_size(axis)
    pairs = [(source, (source + steps) % count) for source in range(count)]
    return lax.ppermute(value, axis, pairs)


def after(value, *earlier):
    return lax.optimization_barrier((value, *earlier))[0]


def issue_order(half):
    hops = half - 1
    plan = (["pair"] + ["scatter"] * hops + ["group"] + ["gather"] * hops) * STEPS
    plan = plan[: len(plan) - hops]
    free = dict.fromkeys(["line", "pair", "group", "core"], 0.0)
    ready = [2.0 * (c // 2) + 0.01 * c for c in range(CHUNKS)]
    at = [0] * CHUNKS
    order = []

    def due(c):
        idle = free["pair"] - OCCUPANCY["pair"] * (len(order) == 1)
        return max(ready[c], idle) if plan[at[c]] == "pair" else ready[c]

    while len(order) < CHUNKS * len(plan):
        c = min((c for c in range(CHUNKS) if at[c] < len(plan)), key=due)
        kind = plan[at[c]]
        link = kind if kind in free else "line"
        free["core"] = max(due(c), free["core"]) + PREPARE[kind]
        start = max(free["core"], free[link])
        free[link] = start + OCCUPANCY[kind]
        ready[c] = free[link] + LATENCY
        at[c] += 1
        order.append(c)
    return order


def shards(tokens, targets, params, momentum, push_weight):
    inputs = tokens[0]
    rows, width = inputs.shape
    features = params.shape[2]
    count = lax.axis_size("fsdp")
    half = count // 2
    block = width // count
    place = lax.div(lax.axis_index("fsdp"), 2)
    lane = lax.rem(lax.axis_index("fsdp"), 2)
    key_scale = width ** (-0.5)
    part = features // CHUNKS
    contract = (((0,), (0,)), ((), ()))
    wide = jnp.float32
    narrow = jnp.bfloat16
    issued = []

    def send(value, link, steps=1):
        if issued:
            value = after(value, issued[-1])
        issued.append(value)
        if link == "pair":
            return lax.ppermute(value, "fsdp", [(i, i ^ 1) for i in range(count)])
        if link == "line":
            return from_behind(value, "fsdp", 2)
        return from_behind(value, "group", steps)

    def chunk(array, c):
        return array[:, c * part : (c + 1) * part]

    def half_columns(source, side):
        pieces = []
        for back in range(half):
            start = (2 * lax.rem(place - back + half, half) + side) * block
            pieces.append(lax.dynamic_slice_in_dim(source, start, block, 1))
        return jnp.concatenate(pieces, axis=1)

    def column_block(back):
        return joined[0][:, back * block : (back + 1) * block]

    outgoing = half_columns(inputs, 1 - lane)
    theirs = lax.ppermute(outgoing, "fsdp", [(i, i ^ 1) for i in range(count)])
    params = after(params, outgoing)
    momentum = after(momentum, outgoing)
    zero = jnp.zeros((), lane.dtype)
    mine = half_columns(after(inputs, outgoing), lane)

    def in_lane_order(own, other):
        both = jnp.zeros((2 * rows, own.shape[1]), own.dtype)
        both = lax.dynamic_update_slice(both, own, (lane * rows, zero))
        return lax.dynamic_update_slice(both, other, ((1 - lane) * rows, zero))

    joined = []
    pair_targets = lax.dynamic_update_slice(
        jnp.zeros((2 * rows, features), targets.dtype), targets[0], (lane * rows, zero)
    )
    held = params.shape[1]
    results = [jnp.zeros_like(params[0]), jnp.zeros_like(momentum[0])]
    weights = [jnp.broadcast_to(push_weight, (1, features))]
    kept, passed = [], []

    def debias(state, weight):
        return (state / weight).astype(narrow)

    def exchange_kept(whole, step):
        kept.append(whole)
        if step == 0:
            extra = jnp.broadcast_to(weights[0], (8, features))
        else:
            left = jnp.broadcast_to(weights[step], (16, features))
            parts = []
            for _ in range(3):
                parts.append(lax.reduce_precision(left, 8, 7))
                left = left - parts[-1]
            row = lax.broadcasted_iota(jnp.int32, (16, features), 0)
            extra = jnp.where(row == 0, parts[0], jnp.where(row == 1, parts[1], parts[2]))
            whole, extra = whole.astype(narrow), extra.astype(narrow)
        whole = jnp.concatenate([whole, extra], axis=0)
        passed.append(send(whole, "group", 2**step) if step else from_behind(whole, "group", 1))

    def read_passed(step):
        got = after(passed[step], issued[-1]).astype(wide)
        passed[step] = got[:held]
        came = got[held : held + 1]
        if step > 0:
            came = came + got[held + 1 : held + 2] + got[held + 2 : held + 3]
        weights.append(0.5 * weights[step] + 0.5 * came)

    first = [[debias(chunk(params[0], c), push_weight[0])] for c in range(CHUNKS)]
    for back in range(1, half):
        for c in range(CHUNKS):
            first[c].append(from_behind(first[c][-1], "fsdp", 2))
        if back == 1:
            exchange_kept(params[0] - (0.2 * 0.9) * momentum[0], 0)
    first_keys = []

    def multiply_first():
        c = len(first_keys)
        both = []
        for pieces in first[c : c + 2]:
            last = after(pieces[-1], issued[-1]) if issued else pieces[-1]
            both.append(jnp.concatenate(pieces[:-1] + [last], axis=0))
        both = after(jnp.concatenate(both, axis=1))
        if joined:
            both = jnp.dot(joined[0], both, preferred_element_type=wide)
        else:
            both = in_lane_order(
                jnp.dot(mine, both, preferred_element_type=wide),
                jnp.dot(theirs, both, preferred_element_type=wide),
            )
        first_keys.extend([both[:, :part], both[:, part:]])

    multiply_first()
    later = []

    def stream(c):
        moment = chunk(momentum[0], c)
        target = chunk(pair_targets, c).astype(wide)
        keys = first_keys[c]
        for step in range(STEPS):
            residual = key_scale * keys - target
            received = yield residual.astype(narrow), "pair"
            grad_out = (key_scale * (residual + received.astype(wide))).astype(narrow)

            def partial(back):
                return lax.dot_general(
                    column_block(back), grad_out, contract, preferred_element_type=wide
                )

            total = partial(1)
            for back in range(2, half + 1):
                arrived = yield total.astype(narrow), "line"
                if step > 0 and c == 0 and back == half:
                    read_passed(step)
                total = arrived.astype(wide) + partial(back % half)
            behind = yield total.astype(narrow), "group"
            moment = 0.9 * moment + total
            mixed = 0.5 * (chunk(kept[step], c) + chunk(passed[step], c))
            state = mixed - 0.1 * (total + behind.astype(wide))
            if step == STEPS - 1:
                break
            later.append(state - (0.2 * 0.9) * moment)
            pieces = [debias(state, chunk(weights[step + 1], c))]
            for _ in range(half - 1):
                pieces.append((yield pieces[-1], "line"))
            keys = sum(
                jnp.dot(column_block(back), piece, preferred_element_type=wide)
                for back, piece in enumerate(pieces)
            )
        fresh = [state / chunk(weights[STEPS], c), moment]
        for i in range(2):
            results[i] = lax.dynamic_update_slice(results[i], fresh[i], (0, c * part))
        yield None, None

    streams = [stream(c) for c in range(CHUNKS)]
    came = [None] * CHUNKS
    mixings = [0] * CHUNKS
    for c in issue_order(half):
        if came[c] is not None:
            came[c] = after(came[c], issued[-1])
        value, link = streams[c].send(came[c])
        came[c] = send(value, link, 2 ** mixings[c])
        if len(issued) == 2:
            joined.append(in_lane_order(mine, after(theirs, issued[-1])))
            while len(first_keys) < CHUNKS:
                multiply_first()
            read_passed(0)
            issued.append(weights[1])
        mixings[c] += link == "group"
        if len(later) == CHUNKS:
            exchange_kept(jnp.concatenate(later, axis=1), mixings[c])
            later.clear()
    for c in range(CHUNKS):
        streams[c].send(came[c])
    return results[0][None], results[1][None]


def solution(mesh):
    return jax.shard_map(
        shards,
        mesh=mesh,
        in_specs=(
            P("group", "fsdp", None),
            P("group", "fsdp", None),
            P("group", "fsdp", None),
            P("group", "fsdp", None),
            P("group"),
        ),
        out_specs=(P("group", "fsdp", None), P("group", "fsdp", None)),
        check_vma=False,
    )
```
